512 devices in a mesh: row: 32 (over y, z_hi), col: 16 (over x, z_lo, core).
Axes of the slice: x: 4, y: 8, z: 8 (z_hi: 4, z_lo: 2; z = z_hi * 2 + z_lo), core: 2. Of those that a mesh axis runs over, the one named last changes fastest.
Arguments:
- activations: bfloat16 [1024, 8192], P('row', 'col'), may hold values from -6 to 6
- out_grad: bfloat16 [1024, 8192], P('row', 'col'), may hold values from -6 to 6
- gate_pre: bfloat16 [1024, 8192], P('row', 'col'), may hold values from -8 to 8
- up_pre: bfloat16 [1024, 8192], P('row', 'col'), may hold values from -6 to 6
- gate_weight: bfloat16 [8192, 8192], P('row', 'col'), may hold values from -0.0625 to 0.0625
- up_weight: bfloat16 [8192, 8192], P('row', 'col'), may hold values from -0.0625 to 0.0625
- down_weight: bfloat16 [8192, 8192], P('col', 'row'), may hold values from -0.0625 to 0.0625
Outputs:
- input_grad: bfloat16 [1024, 8192], P('row', 'col')
- gate_weight_grad: bfloat16 [8192, 8192], P('row', 'col')
- up_weight_grad: bfloat16 [8192, 8192], P('row', 'col')
- down_weight_grad: bfloat16 [8192, 8192], P('col', 'row')
The draws below stay inside these ranges and needn't reach their ends.
All inputs are finite; a program needn't handle non-finite values.
Results may differ from the reference program's by a relative error of at most 0.005.
Values may be sent and summed in bfloat16 or wider, within the bound.
No kernel may reach another device: no remote copies, remote signals or barrier semaphores. Data moves between devices by JAX's collectives and lax.ppermute only.
A program may use at most 64 MiB of HBM per device.

```python
import jax
import jax.numpy as jnp

D = 8192
FF = 8192
TOKENS = 1024


def spiked(values, key, source, target, parts, factor):
    owner, partner = [(jnp.arange(values.shape[axis_at]) // (values.shape[axis_at] // parts)).reshape([-1 if axis == axis_at else 1 for axis in range(values.ndim)]) for axis_at in (source, target)]
    chosen = jax.random.permutation(key, parts)[partner]
    strong = (owner == chosen) | (owner == (partner + parts // 2) % parts)
    return jnp.where(strong, factor * values, values)


def block_scale(key, dims, pieces, smallest, top_value):
    loudness, own = 1.0, jax.random.fold_in(key, 6)
    for position, shards_of in pieces:
        steps = jnp.exp(jax.random.uniform(jax.random.fold_in(own, position), (shards_of,), jnp.float32, smallest / len(pieces), top_value / len(pieces)))
        loudness = loudness * jnp.repeat(steps, dims[position] // shards_of).reshape([-1 if axis == position else 1 for axis in range(len(dims))])
    return loudness


def centred(own_key, shape, spread, reach, split=(), held_as=jnp.bfloat16):
    entries = jax.random.normal(own_key, shape, jnp.float32) * spread
    if len(split) > 0:
        entries = block_scale(own_key, shape, split, -0.22, 0.18) * entries
    return jnp.clip(entries, min=-reach, max=reach).astype(held_as)


def gaussian_with(rng, shape, spread, most, shards, heavy, kind=jnp.bfloat16):
    drawn = spread * jax.random.normal(rng, shape, jnp.float32)
    if shards:
        drawn = drawn * block_scale(rng, shape, shards, -0.22, 0.18)
    return jnp.clip(spiked(drawn, jax.random.fold_in(rng, 3), *heavy), -most, most).astype(kind)


def setup_inputs(seed: int = 0) -> dict:
    splits = jax.random.split(jax.random.key(seed), 8)
    return {
        "activations": centred(splits[0], (TOKENS, D), 1.0, 6.0, ((0, 32), (1, 16))),
        "out_grad": gaussian_with(splits[1], (TOKENS, D), 1.0, 6.0, ((0, 32), (1, 16)), (1, 0, 32, 2.75)),
        "gate_pre": centred(splits[2], (TOKENS, FF), 1.5, 8.0, ((0, 32), (1, 16))),
        "up_pre": centred(splits[3], (TOKENS, FF), 1.0, 6.0, ((0, 32), (1, 16))),
        "gate_weight": centred(splits[4], (D, FF), D ** -0.5, 0.0625, ((0, 32), (1, 16))),
        "up_weight": centred(splits[5], (D, FF), D ** -0.5, 0.0625, ((0, 32), (1, 16))),
        "down_weight": centred(splits[6], (FF, D), FF ** -0.5, 0.0625, ((0, 16), (1, 32))),
    }


def reference(activations, out_grad, gate_pre, up_pre, gate_weight, up_weight, down_weight):
    gate_float = gate_pre.astype(jnp.float32)
    up_float = up_pre.astype(jnp.float32)
    sigmoid_gate = jax.nn.sigmoid(gate_float)
    activated = gate_float * sigmoid_gate
    hidden = (activated * up_float).astype(jnp.bfloat16)
    hidden_grad = jnp.dot(out_grad, down_weight.T, preferred_element_type=jnp.float32)
    gate_grad = (hidden_grad * up_float * sigmoid_gate * (1.0 + gate_float * (1.0 - sigmoid_gate))).astype(jnp.bfloat16)
    up_grad = (hidden_grad * activated).astype(jnp.bfloat16)
    input_grad = (jnp.dot(gate_grad, gate_weight.T, preferred_element_type=jnp.float32)
                  + jnp.dot(up_grad, up_weight.T, preferred_element_type=jnp.float32)).astype(jnp.bfloat16)
    gate_weight_grad = jnp.dot(activations.T, gate_grad, preferred_element_type=jnp.float32).astype(jnp.bfloat16)
    up_weight_grad = jnp.dot(activations.T, up_grad, preferred_element_type=jnp.float32).astype(jnp.bfloat16)
    down_weight_grad = jnp.dot(hidden.T, out_grad, preferred_element_type=jnp.float32).astype(jnp.bfloat16)
    return input_grad, gate_weight_grad, up_weight_grad, down_weight_grad
```

```python
import jax
import jax.numpy as jnp
from jax import lax
from jax.sharding import Mesh
from jax.sharding import PartitionSpec as P

ROW = ("y", "zh")
COL = ("x", "zl", "core")
ALL = ROW + COL
R, C = 32, 16

SAME = [(t * C + f, (2 * f + t % 2) * C + t // 2) for t in range(R) for f in range(C)]
OTHER = [(t * C + f, (2 * f + 1 - t % 2) * C + t // 2) for t in range(R) for f in range(C)]


def inverse(pairs):
    return [(b, a) for a, b in pairs]


def contract_rows(left, right):
    return lax.dot_general(
        left, right, (((0,), (0,)), ((), ())), preferred_element_type=jnp.float32
    )


def contract_cols(left, right):
    return lax.dot_general(
        left, right, (((1,), (1,)), ((), ())), preferred_element_type=jnp.float32
    )


def to_features(tile, parity):
    low, high = tile[..., :256], tile[..., 256:]
    mine = jnp.where(parity == 0, low, high)
    rest = jnp.where(parity == 0, high, low)
    mine = lax.ppermute(mine, ALL, SAME)
    rest = lax.ppermute(rest, ALL, OTHER)
    first = jnp.where(parity == 0, mine, rest)
    second = jnp.where(parity == 0, rest, mine)
    return jnp.concatenate([first, second], axis=-2)


def to_tokens(piece, parity):
    first, second = piece[:32], piece[32:]
    mine = jnp.where(parity == 0, first, second)
    rest = jnp.where(parity == 0, second, first)
    mine = lax.ppermute(mine, ALL, inverse(SAME))
    rest = lax.ppermute(rest, ALL, inverse(OTHER))
    low = jnp.where(parity == 0, mine, rest)
    high = jnp.where(parity == 0, rest, mine)
    return jnp.concatenate([low, high], axis=1)


def gather_copies(block, axes, size):
    copies = jnp.broadcast_to(block[None], (size,) + block.shape)
    got = lax.all_to_all(copies, axes, 0, 0, tiled=True)
    return got.reshape((size * block.shape[0],) + block.shape[1:])


def scatter_sum(partial, axes, size):
    pieces = partial.astype(jnp.bfloat16).reshape((size, partial.shape[0] // size, partial.shape[1]))
    got = lax.all_to_all(pieces, axes, 0, 0, tiled=True)
    return jnp.sum(got.astype(jnp.float32), axis=0).astype(jnp.bfloat16)


def swiglu_back(hidden_grad, gate_pre, up_pre):
    grad_float = hidden_grad.astype(jnp.float32)
    gate_float = gate_pre.astype(jnp.float32)
    up_float = up_pre.astype(jnp.float32)
    sigmoid_gate = jax.nn.sigmoid(gate_float)
    activated = gate_float * sigmoid_gate
    gate_grad = (
        grad_float * up_float * sigmoid_gate * (1.0 + gate_float * (1.0 - sigmoid_gate))
    ).astype(jnp.bfloat16)
    up_grad = (grad_float * activated).astype(jnp.bfloat16)
    hidden = (activated * up_float).astype(jnp.bfloat16)
    return gate_grad, up_grad, hidden


def local(activations, out_grad, gate_pre, up_pre, gate_weight, up_weight, down_weight):
    parity = lax.axis_index("zh") % 2
    pre = lax.all_gather(jnp.concatenate([gate_pre, up_pre], axis=1), ROW, axis=0, tiled=True)
    pieces = to_features(jnp.stack([out_grad, activations]), parity)
    grad_cols = gather_copies(pieces[0], COL, C)
    token_cols = gather_copies(pieces[1], COL, C)
    hidden_grad = scatter_sum(contract_cols(grad_cols, down_weight), ROW, R)
    hidden_grad = gather_copies(hidden_grad, ROW, R)
    gate_all, up_all, hidden_all = swiglu_back(hidden_grad, pre[:, :512], pre[:, 512:])
    partial_input = contract_cols(gate_all, gate_weight) + contract_cols(up_all, up_weight)
    input_grad = to_tokens(scatter_sum(partial_input, COL, C), parity)
    gate_weight_grad = contract_rows(token_cols, gate_all).astype(jnp.bfloat16)
    up_weight_grad = contract_rows(token_cols, up_all).astype(jnp.bfloat16)
    down_weight_grad = contract_rows(hidden_all, grad_cols).astype(jnp.bfloat16)
    return (input_grad, gate_weight_grad, up_weight_grad, down_weight_grad)


def solution(mesh):
    fine = Mesh(mesh.devices.reshape(8, 4, 4, 2, 2), ALL)
    return jax.shard_map(
        local,
        mesh=fine,
        in_specs=(P(ROW, COL),) * 6 + (P(COL, ROW),),
        out_specs=(P(ROW, COL),) * 3 + (P(COL, ROW),),
        check_vma=False,
    )
```

```python
import jax
import jax.numpy as jnp
from jax import lax
from jax.sharding import Mesh
from jax.sharding import PartitionSpec as P

AXES = ("yh", "yl", "zh", "x", "zl", "core")
ROW = ("yh", "yl", "zh")
HALF = ("yh", "zh")
COL = ("x", "zl", "core")
R, C = 32, 16


def turn_pairs(half_of):
    pairs = []
    for t in range(R):
        yh, yl, zh = t // 8, t // 4 % 2, t % 4
        for f in range(C):
            h = half_of(f // 2 % 2)
            row = (f // 4) * 8 + yl * 4 + (f % 2) * 2 + h
            pairs.append((t * C + f, row * C + yh * 4 + zh))
    return pairs


FIRST = turn_pairs(lambda b: b)
SECOND = turn_pairs(lambda b: 1 - b)


def inverse(pairs):
    return [(b, a) for a, b in pairs]


def contract_rows(left, right):
    return lax.dot_general(
        left, right, (((0,), (0,)), ((), ())), preferred_element_type=jnp.float32
    )


def contract_cols(left, right):
    return lax.dot_general(
        left, right, (((1,), (1,)), ((), ())), preferred_element_type=jnp.float32
    )


def swap(value):
    return lax.ppermute(value, "yl", [(0, 1), (1, 0)])


def choose(flag, one, other):
    return jnp.where(flag, one, other), jnp.where(flag, other, one)


def to_features(tile, upper, mine):
    one, two = choose(upper, tile[..., 256:], tile[..., :256])
    one = lax.ppermute(one, AXES, FIRST)
    two = lax.ppermute(two, AXES, SECOND)
    return choose(mine, one, two)


def to_tokens(own, other, upper, mine):
    one, two = choose(mine, own, other)
    one = lax.ppermute(one, AXES, inverse(FIRST))
    two = lax.ppermute(two, AXES, inverse(SECOND))
    high, low = choose(upper, one, two)
    return jnp.concatenate([low, high], axis=-1)


def gather_copies(block, axes, size):
    copies = jnp.broadcast_to(block[None], (size,) + block.shape)
    got = lax.all_to_all(copies, axes, 0, 0, tiled=True)
    return got.reshape((size * block.shape[0],) + block.shape[1:])


def scatter_sum(partial, axes, size):
    pieces = partial.astype(jnp.bfloat16).reshape((size, partial.shape[0] // size, partial.shape[1]))
    got = lax.all_to_all(pieces, axes, 0, 0, tiled=True)
    return jnp.sum(got.astype(jnp.float32), axis=0).astype(jnp.bfloat16)


def swiglu_back(hidden_grad, gate_pre, up_pre):
    grad_float = hidden_grad.astype(jnp.float32)
    gate_float = gate_pre.astype(jnp.float32)
    up_float = up_pre.astype(jnp.float32)
    sigmoid_gate = jax.nn.sigmoid(gate_float)
    activated = gate_float * sigmoid_gate
    gate_grad = (
        grad_float * up_float * sigmoid_gate * (1.0 + gate_float * (1.0 - sigmoid_gate))
    ).astype(jnp.bfloat16)
    up_grad = (grad_float * activated).astype(jnp.bfloat16)
    hidden = (activated * up_float).astype(jnp.bfloat16)
    return gate_grad, up_grad, hidden


def local(activations, out_grad, gate_pre, up_pre, gate_weight, up_weight, down_weight):
    upper = lax.axis_index("zl") == 1
    mine = lax.axis_index("zh") % 2 == lax.axis_index("yl")
    own, other = to_features(jnp.stack([out_grad, activations]), upper, mine)
    pre = jnp.concatenate([gate_pre, up_pre], axis=1)
    pre = jnp.concatenate([pre, swap(pre)], axis=1)
    pre = lax.all_gather(pre, HALF, axis=0, tiled=True)
    grads = gather_copies(jnp.concatenate([own[0], other[0]], axis=1), COL, C)
    swapped = swap(other)
    cols = jnp.concatenate([own[1], swapped[1], own[0], swapped[0]], axis=1)
    cols = lax.all_gather(cols, COL, axis=0, tiled=True)
    down_other = swap(down_weight)
    gate_other, up_other = swap(gate_weight), swap(up_weight)

    partial = contract_cols(grads[:, :256], down_weight) + contract_cols(grads[:, 256:], down_other)
    hidden_grad = scatter_sum(partial, HALF, C)
    hidden_grad, pre = lax.optimization_barrier((hidden_grad, pre))
    hidden_grad = gather_copies(hidden_grad, HALF, C)
    gate_a, up_a, hidden_a = swiglu_back(hidden_grad, pre[:, :512], pre[:, 512:1024])
    swapped_grad, pre, cols = lax.optimization_barrier((swap(hidden_grad), pre, cols))
    gate_b, up_b, hidden_b = swiglu_back(swapped_grad, pre[:, 1024:1536], pre[:, 1536:])
    partial = jnp.concatenate(
        [
            contract_cols(gate_a, gate_weight) + contract_cols(up_a, up_weight),
            contract_cols(gate_a, gate_other) + contract_cols(up_a, up_other),
        ],
        axis=1,
    )
    summed = scatter_sum(partial, COL, C)
    input_grad = to_tokens(summed[:, :256], summed[:, 256:], upper, mine)
    tokens_a, tokens_b = cols[:, :256], cols[:, 256:512]
    grads_a, grads_b = cols[:, 512:768], cols[:, 768:]
    gate_weight_grad = contract_rows(tokens_a, gate_a) + contract_rows(tokens_b, gate_b)
    up_weight_grad = contract_rows(tokens_a, up_a) + contract_rows(tokens_b, up_b)
    down_weight_grad = contract_rows(hidden_a, grads_a) + contract_rows(hidden_b, grads_b)
    return (
        input_grad,
        gate_weight_grad.astype(jnp.bfloat16),
        up_weight_grad.astype(jnp.bfloat16),
        down_weight_grad.astype(jnp.bfloat16),
    )


def solution(mesh):
    fine = Mesh(mesh.devices.reshape(4, 2, 4, 4, 2, 2), AXES)
    return jax.shard_map(
        local,
        mesh=fine,
        in_specs=(P(ROW, COL),) * 6 + (P(COL, ROW),),
        out_specs=(P(ROW, COL),) * 3 + (P(COL, ROW),),
        check_vma=False,
    )
```

```python
import jax
import jax.numpy as jnp
from jax import lax
from jax.sharding import Mesh
from jax.sharding import PartitionSpec as P

AXES = ("yh", "yl", "zh", "x", "zl", "core")
ROW = ("yh", "yl", "zh")
HALF = ("yh", "zh")
COL = ("x", "zl", "core")
R, C = 32, 16


def turn_pairs(half_of):
    pairs = []
    for t in range(R):
        yh, yl, zh = t // 8, t // 4 % 2, t % 4
        for f in range(C):
            h = half_of(f // 2 % 2)
            row = (f // 4) * 8 + yl * 4 + (f % 2) * 2 + h
            pairs.append((t * C + f, row * C + yh * 4 + zh))
    return pairs


FIRST = turn_pairs(lambda b: b)
SECOND = turn_pairs(lambda b: 1 - b)


def inverse(pairs):
    return [(b, a) for a, b in pairs]


def contract_rows(left, right):
    return lax.dot_general(
        left, right, (((0,), (0,)), ((), ())), preferred_element_type=jnp.float32
    )


def contract_cols(left, right):
    return lax.dot_general(
        left, right, (((1,), (1,)), ((), ())), preferred_element_type=jnp.float32
    )


def swap(value):
    return lax.ppermute(value, "yl", [(0, 1), (1, 0)])


def choose(flag, one, other):
    return jnp.where(flag, one, other), jnp.where(flag, other, one)


def halves(value):
    parts = value.reshape((4, 2, value.shape[0] // 8, value.shape[1]))
    yl = lax.axis_index("yl")
    return tuple(
        lax.dynamic_index_in_dim(parts, at, 1, keepdims=False).reshape((-1, value.shape[1]))
        for at in (yl, 1 - yl)
    )


def to_features(tile, upper, mine):
    one, two = choose(upper, tile[..., 256:], tile[..., :256])
    one = lax.ppermute(one, AXES, FIRST)
    two = lax.ppermute(two, AXES, SECOND)
    return choose(mine, one, two)


def to_tokens(own, other, upper, mine):
    one, two = choose(mine, own, other)
    one = lax.ppermute(one, AXES, inverse(FIRST))
    two = lax.ppermute(two, AXES, inverse(SECOND))
    high, low = choose(upper, one, two)
    return jnp.concatenate([low, high], axis=-1)


def gather_copies(block, axes, size):
    copies = jnp.broadcast_to(block[None], (size,) + block.shape)
    got = lax.all_to_all(copies, axes, 0, 0, tiled=True)
    return got.reshape((size * block.shape[0],) + block.shape[1:])


def scatter_sum(partial, axes, size):
    pieces = partial.astype(jnp.bfloat16).reshape((size, partial.shape[0] // size, partial.shape[1]))
    got = lax.all_to_all(pieces, axes, 0, 0, tiled=True)
    return jnp.sum(got.astype(jnp.float32), axis=0).astype(jnp.bfloat16)


def swiglu_back(hidden_grad, gate_pre, up_pre):
    grad_float = hidden_grad.astype(jnp.float32)
    gate_float = gate_pre.astype(jnp.float32)
    up_float = up_pre.astype(jnp.float32)
    sigmoid_gate = jax.nn.sigmoid(gate_float)
    activated = gate_float * sigmoid_gate
    gate_grad = (
        grad_float * up_float * sigmoid_gate * (1.0 + gate_float * (1.0 - sigmoid_gate))
    ).astype(jnp.bfloat16)
    up_grad = (grad_float * activated).astype(jnp.bfloat16)
    hidden = (activated * up_float).astype(jnp.bfloat16)
    return gate_grad, up_grad, hidden


def local(activations, out_grad, gate_pre, up_pre, gate_weight, up_weight, down_weight):
    upper = lax.axis_index("zl") == 1
    mine = lax.axis_index("zh") % 2 == lax.axis_index("yl")
    pre = gather_copies(jnp.concatenate([gate_pre, up_pre], axis=1), "zh", 4)
    tiles = to_features(jnp.stack([out_grad, activations]), upper, mine)
    (own, other), pre = lax.optimization_barrier((tiles, pre))
    pre = lax.all_gather(pre, ("yh", "yl"), axis=0, tiled=True)
    grads = gather_copies(jnp.concatenate([own[0], other[0]], axis=1), COL, C)
    swapped = swap(other)
    cols = jnp.concatenate([own[1], swapped[1], own[0], swapped[0]], axis=1)
    cols = lax.all_gather(cols, COL, axis=0, tiled=True)
    down_other = swap(down_weight)
    gate_other, up_other = swap(gate_weight), swap(up_weight)

    partial = contract_cols(grads[:, :256], down_weight) + contract_cols(grads[:, 256:], down_other)
    partial, gate_other, up_other = lax.optimization_barrier(
        (partial.astype(jnp.bfloat16), gate_other, up_other)
    )
    hidden_grad = scatter_sum(partial, HALF, C)
    hidden_grad, pre, cols = lax.optimization_barrier((hidden_grad, pre, cols))
    hidden_grad = gather_copies(hidden_grad, HALF, C)
    pre_a, pre_b = halves(pre)
    gate_a, up_a, hidden_a = swiglu_back(hidden_grad, pre_a[:, :512], pre_a[:, 512:])
    swapped_grad, pre_b, cols = lax.optimization_barrier((swap(hidden_grad), pre_b, cols))
    gate_b, up_b, hidden_b = swiglu_back(swapped_grad, pre_b[:, :512], pre_b[:, 512:])
    partial = jnp.concatenate(
        [
            contract_cols(gate_a, gate_weight) + contract_cols(up_a, up_weight),
            contract_cols(gate_a, gate_other) + contract_cols(up_a, up_other),
        ],
        axis=1,
    )
    summed = scatter_sum(partial, COL, C)
    input_grad = to_tokens(summed[:, :256], summed[:, 256:], upper, mine)
    tokens_a, tokens_b = cols[:, :256], cols[:, 256:512]
    grads_a, grads_b = cols[:, 512:768], cols[:, 768:]
    gate_weight_grad = contract_rows(tokens_a, gate_a) + contract_rows(tokens_b, gate_b)
    up_weight_grad = contract_rows(tokens_a, up_a) + contract_rows(tokens_b, up_b)
    down_weight_grad = contract_rows(hidden_a, grads_a) + contract_rows(hidden_b, grads_b)
    return (
        input_grad,
        gate_weight_grad.astype(jnp.bfloat16),
        up_weight_grad.astype(jnp.bfloat16),
        down_weight_grad.astype(jnp.bfloat16),
    )


def solution(mesh):
    fine = Mesh(mesh.devices.reshape(4, 2, 4, 4, 2, 2), AXES)
    return jax.shard_map(
        local,
        mesh=fine,
        in_specs=(P(ROW, COL),) * 6 + (P(COL, ROW),),
        out_specs=(P(ROW, COL),) * 3 + (P(COL, ROW),),
        check_vma=False,
    )
```

```python
import jax
import jax.numpy as jnp
from jax import lax
from jax.sharding import Mesh
from jax.sharding import PartitionSpec as P

AXES = ("yh", "yl", "zh", "x", "zl", "core")
ROW = ("yh", "yl", "zh")
HALF = ("yh", "zh")
COL = ("x", "zl", "core")
R, C = 32, 16


def turn_pairs(half_of):
    pairs = []
    for t in range(R):
        yh, yl, zh = t // 8, t // 4 % 2, t % 4
        for f in range(C):
            h = half_of(f // 2 % 2)
            row = (f // 4) * 8 + yl * 4 + (f % 2) * 2 + h
            pairs.append((t * C + f, row * C + yh * 4 + zh))
    return pairs


FIRST = turn_pairs(lambda b: b)
SECOND = turn_pairs(lambda b: 1 - b)


def inverse(pairs):
    return [(b, a) for a, b in pairs]


def contract_rows(left, right):
    return lax.dot_general(
        left, right, (((0,), (0,)), ((), ())), preferred_element_type=jnp.float32
    )


def contract_cols(left, right):
    return lax.dot_general(
        left, right, (((1,), (1,)), ((), ())), preferred_element_type=jnp.float32
    )


def swap(value):
    return lax.ppermute(value, "yl", [(0, 1), (1, 0)])


def choose(flag, one, other):
    return jnp.where(flag, one, other), jnp.where(flag, other, one)


def halves(value):
    parts = value.reshape((4, 2, value.shape[0] // 8, value.shape[1]))
    yl = lax.axis_index("yl")
    return tuple(
        lax.dynamic_index_in_dim(parts, at, 1, keepdims=False).reshape((-1, value.shape[1]))
        for at in (yl, 1 - yl)
    )


def to_features(tile, upper, mine):
    one, two = choose(upper, tile[..., 256:], tile[..., :256])
    one = lax.ppermute(one, AXES, FIRST)
    two = lax.ppermute(two, AXES, SECOND)
    return choose(mine, one, two)


def to_tokens(own, other, upper, mine):
    one, two = choose(mine, own, other)
    one = lax.ppermute(one, AXES, inverse(FIRST))
    two = lax.ppermute(two, AXES, inverse(SECOND))
    high, low = choose(upper, one, two)
    return jnp.concatenate([low, high], axis=-1)


def gather_copies(block, axes, size):
    copies = jnp.broadcast_to(block[None], (size,) + block.shape)
    got = lax.all_to_all(copies, axes, 0, 0, tiled=True)
    return got.reshape((size * block.shape[0],) + block.shape[1:])


def scatter_sum(partial, axes, size):
    pieces = partial.astype(jnp.bfloat16).reshape((size, partial.shape[0] // size, partial.shape[1]))
    got = lax.all_to_all(pieces, axes, 0, 0, tiled=True)
    return jnp.sum(got.astype(jnp.float32), axis=0).astype(jnp.bfloat16)


def swiglu_back(hidden_grad, gate_pre, up_pre):
    grad_float = hidden_grad.astype(jnp.float32)
    gate_float = gate_pre.astype(jnp.float32)
    up_float = up_pre.astype(jnp.float32)
    sigmoid_gate = jax.nn.sigmoid(gate_float)
    activated = gate_float * sigmoid_gate
    gate_grad = (
        grad_float * up_float * sigmoid_gate * (1.0 + gate_float * (1.0 - sigmoid_gate))
    ).astype(jnp.bfloat16)
    up_grad = (grad_float * activated).astype(jnp.bfloat16)
    hidden = (activated * up_float).astype(jnp.bfloat16)
    return gate_grad, up_grad, hidden


def local(activations, out_grad, gate_pre, up_pre, gate_weight, up_weight, down_weight):
    upper = lax.axis_index("zl") == 1
    mine = lax.axis_index("zh") % 2 == lax.axis_index("yl")
    pre = gather_copies(jnp.concatenate([gate_pre, up_pre], axis=1), "zh", 4)
    tiles = to_features(jnp.stack([out_grad, activations]), upper, mine)
    (own, other), pre = lax.optimization_barrier((tiles, pre))
    pre = lax.all_gather(pre, ("yh", "yl"), axis=0, tiled=True)
    grads = gather_copies(jnp.concatenate([own[0], other[0]], axis=1), COL, C)
    swapped = swap(other)
    cols = jnp.concatenate([own[1], swapped[1], own[0], swapped[0]], axis=1)
    down_other = swap(down_weight)
    gate_other, up_other = swap(gate_weight), swap(up_weight)

    partial = contract_cols(grads[:, :256], down_weight) + contract_cols(grads[:, 256:], down_other)
    partial, cols = lax.optimization_barrier((partial.astype(jnp.bfloat16), cols))
    cols = lax.all_gather(cols, COL, axis=0, tiled=True)
    hidden_grad = scatter_sum(partial, HALF, C)
    hidden_grad, pre = lax.optimization_barrier((hidden_grad, pre))
    hidden_grad = gather_copies(hidden_grad, HALF, C)
    hidden_grad, cols = lax.optimization_barrier((hidden_grad, cols))
    pre_a, pre_b = halves(pre)
    gate_a, up_a, hidden_a = swiglu_back(hidden_grad, pre_a[:, :512], pre_a[:, 512:])
    swapped_grad, pre_b, cols = lax.optimization_barrier((swap(hidden_grad), pre_b, cols))
    gate_b, up_b, hidden_b = swiglu_back(swapped_grad, pre_b[:, :512], pre_b[:, 512:])
    partial = jnp.concatenate(
        [
            contract_cols(gate_a, gate_weight) + contract_cols(up_a, up_weight),
            contract_cols(gate_a, gate_other) + contract_cols(up_a, up_other),
        ],
        axis=1,
    )
    summed = scatter_sum(partial, COL, C)
    input_grad = to_tokens(summed[:, :256], summed[:, 256:], upper, mine)
    tokens_a, tokens_b = cols[:, :256], cols[:, 256:512]
    grads_a, grads_b = cols[:, 512:768], cols[:, 768:]
    gate_weight_grad = contract_rows(tokens_a, gate_a) + contract_rows(tokens_b, gate_b)
    up_weight_grad = contract_rows(tokens_a, up_a) + contract_rows(tokens_b, up_b)
    down_weight_grad = contract_rows(hidden_a, grads_a) + contract_rows(hidden_b, grads_b)
    return (
        input_grad,
        gate_weight_grad.astype(jnp.bfloat16),
        up_weight_grad.astype(jnp.bfloat16),
        down_weight_grad.astype(jnp.bfloat16),
    )


def solution(mesh):
    fine = Mesh(mesh.devices.reshape(4, 2, 4, 4, 2, 2), AXES)
    return jax.shard_map(
        local,
        mesh=fine,
        in_specs=(P(ROW, COL),) * 6 + (P(COL, ROW),),
        out_specs=(P(ROW, COL),) * 3 + (P(COL, ROW),),
        check_vma=False,
    )
```

```python
import jax
import jax.numpy as jnp
from jax import lax
from jax.sharding import Mesh
from jax.sharding import PartitionSpec as P

AXES = ("yh", "yl", "zh", "x", "zl", "core")
ROW = ("yh", "yl", "zh")
HALF = ("yh", "zh")
COL = ("x", "zl", "core")
R, C = 32, 16


def turn_pairs(half_of):
    pairs = []
    for t in range(R):
        yh, yl, zh = t // 8, t // 4 % 2, t % 4
        for f in range(C):
            h = half_of(f // 2 % 2)
            row = (f // 4) * 8 + yl * 4 + (f % 2) * 2 + h
            pairs.append((t * C + f, row * C + yh * 4 + zh))
    return pairs


FIRST = turn_pairs(lambda b: b)
SECOND = turn_pairs(lambda b: 1 - b)


def inverse(pairs):
    return [(b, a) for a, b in pairs]


def contract_rows(left, right):
    return lax.dot_general(
        left, right, (((0,), (0,)), ((), ())), preferred_element_type=jnp.float32
    )


def contract_cols(left, right):
    return lax.dot_general(
        left, right, (((1,), (1,)), ((), ())), preferred_element_type=jnp.float32
    )


def swap(value):
    return lax.ppermute(value, "yl", [(0, 1), (1, 0)])


def choose(flag, one, other):
    return jnp.where(flag, one, other), jnp.where(flag, other, one)


def halves(value):
    parts = value.reshape((4, 2, value.shape[0] // 8, value.shape[1]))
    yl = lax.axis_index("yl")
    return tuple(
        lax.dynamic_index_in_dim(parts, at, 1, keepdims=False).reshape((-1, value.shape[1]))
        for at in (yl, 1 - yl)
    )


def to_features(tile, upper, mine):
    one, two = choose(upper, tile[..., 256:], tile[..., :256])
    one = lax.ppermute(one, AXES, FIRST)
    two = lax.ppermute(two, AXES, SECOND)
    return choose(mine, one, two)


def to_tokens(own, other, upper, mine):
    one, two = choose(mine, own, other)
    one = lax.ppermute(one, AXES, inverse(FIRST))
    two = lax.ppermute(two, AXES, inverse(SECOND))
    high, low = choose(upper, one, two)
    return jnp.concatenate([low, high], axis=-1)


def gather_copies(block, axes, size):
    copies = jnp.broadcast_to(block[None], (size,) + block.shape)
    got = lax.all_to_all(copies, axes, 0, 0, tiled=True)
    return got.reshape((size * block.shape[0],) + block.shape[1:])


def scatter_sum(partial, axes, size):
    pieces = partial.astype(jnp.bfloat16).reshape((size, partial.shape[0] // size, partial.shape[1]))
    got = lax.all_to_all(pieces, axes, 0, 0, tiled=True)
    return jnp.sum(got.astype(jnp.float32), axis=0).astype(jnp.bfloat16)


def swiglu_back(hidden_grad, gate_pre, up_pre):
    grad_float = hidden_grad.astype(jnp.float32)
    gate_float = gate_pre.astype(jnp.float32)
    up_float = up_pre.astype(jnp.float32)
    sigmoid_gate = jax.nn.sigmoid(gate_float)
    activated = gate_float * sigmoid_gate
    gate_grad = (
        grad_float * up_float * sigmoid_gate * (1.0 + gate_float * (1.0 - sigmoid_gate))
    ).astype(jnp.bfloat16)
    up_grad = (grad_float * activated).astype(jnp.bfloat16)
    hidden = (activated * up_float).astype(jnp.bfloat16)
    return gate_grad, up_grad, hidden


def local(activations, out_grad, gate_pre, up_pre, gate_weight, up_weight, down_weight):
    upper = lax.axis_index("zl") == 1
    mine = lax.axis_index("zh") % 2 == lax.axis_index("yl")
    pre = gather_copies(jnp.concatenate([gate_pre, up_pre], axis=1), "zh", 4)
    tiles = to_features(jnp.stack([out_grad, activations]), upper, mine)
    (own, other), pre, down_other = lax.optimization_barrier((tiles, pre, swap(down_weight)))
    pre = lax.all_gather(pre, ("yh", "yl"), axis=0, tiled=True)
    cols = jnp.concatenate([own[0], other[0], other[1], own[1]], axis=1)
    cols = gather_copies(cols, COL, C)
    grads_a, grads_other, tokens_a = cols[:, :256], cols[:, 256:512], cols[:, 768:]
    gate_other, up_other = swap(gate_weight), swap(up_weight)

    partial = contract_cols(grads_a, down_weight) + contract_cols(grads_other, down_other)
    hidden_grad = scatter_sum(partial, HALF, C)
    hidden_grad, pre, gate_other, up_other = lax.optimization_barrier(
        (hidden_grad, pre, gate_other, up_other)
    )
    hidden_grad = gather_copies(hidden_grad, HALF, C)
    pre_a, pre_b = halves(pre)
    gate_a, up_a, hidden_a = swiglu_back(hidden_grad, pre_a[:, :512], pre_a[:, 512:])
    swapped_grad, pre_b = lax.optimization_barrier((swap(hidden_grad), pre_b))
    gate_b, up_b, hidden_b = swiglu_back(swapped_grad, pre_b[:, :512], pre_b[:, 512:])
    partial = jnp.concatenate(
        [
            contract_cols(gate_a, gate_weight) + contract_cols(up_a, up_weight),
            contract_cols(gate_a, gate_other) + contract_cols(up_a, up_other),
        ],
        axis=1,
    )
    summed = scatter_sum(partial, COL, C)
    input_grad = to_tokens(summed[:, :256], summed[:, 256:], upper, mine)
    swapped_cols = swap(cols[:, 256:768])
    grads_b, tokens_b = swapped_cols[:, :256], swapped_cols[:, 256:]
    gate_weight_grad = contract_rows(tokens_a, gate_a) + contract_rows(tokens_b, gate_b)
    up_weight_grad = contract_rows(tokens_a, up_a) + contract_rows(tokens_b, up_b)
    down_weight_grad = contract_rows(hidden_a, grads_a) + contract_rows(hidden_b, grads_b)
    return (
        input_grad,
        gate_weight_grad.astype(jnp.bfloat16),
        up_weight_grad.astype(jnp.bfloat16),
        down_weight_grad.astype(jnp.bfloat16),
    )


def solution(mesh):
    fine = Mesh(mesh.devices.reshape(4, 2, 4, 4, 2, 2), AXES)
    return jax.shard_map(
        local,
        mesh=fine,
        in_specs=(P(ROW, COL),) * 6 + (P(COL, ROW),),
        out_specs=(P(ROW, COL),) * 3 + (P(COL, ROW),),
        check_vma=False,
    )
```

```python
import jax
import jax.numpy as jnp
from jax import lax
from jax.sharding import Mesh
from jax.sharding import PartitionSpec as P

AXES = ("yh", "yl", "zh", "x", "zl", "core")
ROW = ("yh", "yl", "zh")
HALF = ("yh", "zh")
COL = ("x", "zl", "core")
R, C = 32, 16


def turn_pairs(half_of):
    pairs = []
    for t in range(R):
        yh, yl, zh = t // 8, t // 4 % 2, t % 4
        for f in range(C):
            h = half_of(f // 2 % 2)
            row = (f // 4) * 8 + yl * 4 + (f % 2) * 2 + h
            pairs.append((t * C + f, row * C + yh * 4 + zh))
    return pairs


FIRST = turn_pairs(lambda b: b)
SECOND = turn_pairs(lambda b: 1 - b)


def inverse(pairs):
    return [(b, a) for a, b in pairs]


def contract_rows(left, right):
    return lax.dot_general(
        left, right, (((0,), (0,)), ((), ())), preferred_element_type=jnp.float32
    )


def contract_cols(left, right):
    return lax.dot_general(
        left, right, (((1,), (1,)), ((), ())), preferred_element_type=jnp.float32
    )


def swap(value):
    return lax.ppermute(value, "yl", [(0, 1), (1, 0)])


def choose(flag, one, other):
    return jnp.where(flag, one, other), jnp.where(flag, other, one)


def halves(value):
    parts = value.reshape((4, 2, value.shape[0] // 8, value.shape[1]))
    yl = lax.axis_index("yl")
    return tuple(
        lax.dynamic_index_in_dim(parts, at, 1, keepdims=False).reshape((-1, value.shape[1]))
        for at in (yl, 1 - yl)
    )


def to_features(tile, upper, mine):
    one, two = choose(upper, tile[..., 256:], tile[..., :256])
    one = lax.ppermute(one, AXES, FIRST)
    two = lax.ppermute(two, AXES, SECOND)
    return choose(mine, one, two)


def to_tokens(own, other, upper, mine):
    one, two = choose(mine, own, other)
    one = lax.ppermute(one, AXES, inverse(FIRST))
    two = lax.ppermute(two, AXES, inverse(SECOND))
    high, low = choose(upper, one, two)
    return jnp.concatenate([low, high], axis=-1)


def gather_copies(block, axes, size):
    copies = jnp.broadcast_to(block[None], (size,) + block.shape)
    got = lax.all_to_all(copies, axes, 0, 0, tiled=True)
    return got.reshape((size * block.shape[0],) + block.shape[1:])


def scatter_sum(partial, axes, size):
    pieces = partial.astype(jnp.bfloat16).reshape((size, partial.shape[0] // size, partial.shape[1]))
    got = lax.all_to_all(pieces, axes, 0, 0, tiled=True)
    return jnp.sum(got.astype(jnp.float32), axis=0).astype(jnp.bfloat16)


def swiglu_back(hidden_grad, gate_pre, up_pre):
    grad_float = hidden_grad.astype(jnp.float32)
    gate_float = gate_pre.astype(jnp.float32)
    up_float = up_pre.astype(jnp.float32)
    sigmoid_gate = jax.nn.sigmoid(gate_float)
    activated = gate_float * sigmoid_gate
    gate_grad = (
        grad_float * up_float * sigmoid_gate * (1.0 + gate_float * (1.0 - sigmoid_gate))
    ).astype(jnp.bfloat16)
    up_grad = (grad_float * activated).astype(jnp.bfloat16)
    hidden = (activated * up_float).astype(jnp.bfloat16)
    return gate_grad, up_grad, hidden


def local(activations, out_grad, gate_pre, up_pre, gate_weight, up_weight, down_weight):
    upper = lax.axis_index("zl") == 1
    mine = lax.axis_index("zh") % 2 == lax.axis_index("yl")
    pre = gather_copies(jnp.concatenate([gate_pre, up_pre], axis=1), "zh", 4)
    tiles = to_features(jnp.stack([out_grad, activations]), upper, mine)
    (own, other), pre, down_other = lax.optimization_barrier((tiles, pre, swap(down_weight)))
    pre = lax.all_gather(pre, ("yh", "yl"), axis=0, tiled=True)
    cols = jnp.concatenate([own[0], other[0], other[1], own[1]], axis=1)
    cols = gather_copies(cols, COL, C)
    grads_a, grads_other, tokens_a = cols[:, :256], cols[:, 256:512], cols[:, 768:]
    gate_other, up_other = swap(gate_weight), swap(up_weight)

    partial = contract_cols(grads_a, down_weight) + contract_cols(grads_other, down_other)
    partial, gate_other, up_other = lax.optimization_barrier(
        (partial.astype(jnp.bfloat16), gate_other, up_other)
    )
    hidden_grad = scatter_sum(partial, HALF, C)
    hidden_grad, pre = lax.optimization_barrier((hidden_grad, pre))
    hidden_grad = gather_copies(hidden_grad, HALF, C)
    pre_a, pre_b = halves(pre)
    gate_a, up_a, hidden_a = swiglu_back(hidden_grad, pre_a[:, :512], pre_a[:, 512:])
    swapped_grad, pre_b = lax.optimization_barrier((swap(hidden_grad), pre_b))
    gate_b, up_b, hidden_b = swiglu_back(swapped_grad, pre_b[:, :512], pre_b[:, 512:])
    partial = jnp.concatenate(
        [
            contract_cols(gate_a, gate_weight) + contract_cols(up_a, up_weight),
            contract_cols(gate_a, gate_other) + contract_cols(up_a, up_other),
        ],
        axis=1,
    )
    summed = scatter_sum(partial, COL, C)
    input_grad = to_tokens(summed[:, :256], summed[:, 256:], upper, mine)
    (cols_other, _) = lax.optimization_barrier((cols[:, 256:768], gate_a))
    swapped_cols = swap(cols_other)
    grads_b, tokens_b = swapped_cols[:, :256], swapped_cols[:, 256:]
    gate_weight_grad = contract_rows(tokens_a, gate_a) + contract_rows(tokens_b, gate_b)
    up_weight_grad = contract_rows(tokens_a, up_a) + contract_rows(tokens_b, up_b)
    down_weight_grad = contract_rows(hidden_a, grads_a) + contract_rows(hidden_b, grads_b)
    return (
        input_grad,
        gate_weight_grad.astype(jnp.bfloat16),
        up_weight_grad.astype(jnp.bfloat16),
        down_weight_grad.astype(jnp.bfloat16),
    )


def solution(mesh):
    fine = Mesh(mesh.devices.reshape(4, 2, 4, 4, 2, 2), AXES)
    return jax.shard_map(
        local,
        mesh=fine,
        in_specs=(P(ROW, COL),) * 6 + (P(COL, ROW),),
        out_specs=(P(ROW, COL),) * 3 + (P(COL, ROW),),
        check_vma=False,
    )
```

```python
import jax
import jax.numpy as jnp
from jax import lax
from jax.sharding import Mesh
from jax.sharding import PartitionSpec as P

AXES = ("y", "zh", "x", "zl", "core")
ROW = ("y", "zh")
COL = ("x", "zl", "core")
PLANE = ("x", "zl")
R, C = 32, 16

SAME = [(t * C + f, (2 * f + t % 2) * C + t // 2) for t in range(R) for f in range(C)]
OTHER = [(t * C + f, (2 * f + 1 - t % 2) * C + t // 2) for t in range(R) for f in range(C)]


def inverse(pairs):
    return [(b, a) for a, b in pairs]


def contract_rows(left, right):
    return lax.dot_general(
        left, right, (((0,), (0,)), ((), ())), preferred_element_type=jnp.float32
    )


def contract_cols(left, right):
    return lax.dot_general(
        left, right, (((1,), (1,)), ((), ())), preferred_element_type=jnp.float32
    )


def swap(value):
    return lax.ppermute(value, "core", [(0, 1), (1, 0)])


def choose(flag, one, other):
    return jnp.where(flag, one, other), jnp.where(flag, other, one)


def to_features(tile, odd):
    one, two = choose(odd, tile[..., 256:], tile[..., :256])
    one = lax.ppermute(one, AXES, SAME)
    two = lax.ppermute(two, AXES, OTHER)
    second, first = choose(odd, one, two)
    return jnp.concatenate([first, second], axis=-2)


def to_tokens(piece, odd):
    one, two = choose(odd, piece[32:], piece[:32])
    one = lax.ppermute(one, AXES, inverse(SAME))
    two = lax.ppermute(two, AXES, inverse(OTHER))
    high, low = choose(odd, one, two)
    return jnp.concatenate([low, high], axis=1)


def gather_copies(block, axes, size):
    copies = jnp.broadcast_to(block[None], (size,) + block.shape)
    got = lax.all_to_all(copies, axes, 0, 0, tiled=True)
    return got.reshape((size * block.shape[0],) + block.shape[1:])


def scatter_sum(partial, axes, size):
    pieces = partial.astype(jnp.bfloat16).reshape((size, partial.shape[0] // size, partial.shape[1]))
    got = lax.all_to_all(pieces, axes, 0, 0, tiled=True)
    return jnp.sum(got.astype(jnp.float32), axis=0).astype(jnp.bfloat16)


def swiglu_back(hidden_grad, gate_pre, up_pre):
    grad_float = hidden_grad.astype(jnp.float32)
    gate_float = gate_pre.astype(jnp.float32)
    up_float = up_pre.astype(jnp.float32)
    sigmoid_gate = jax.nn.sigmoid(gate_float)
    activated = gate_float * sigmoid_gate
    gate_grad = (
        grad_float * up_float * sigmoid_gate * (1.0 + gate_float * (1.0 - sigmoid_gate))
    ).astype(jnp.bfloat16)
    up_grad = (grad_float * activated).astype(jnp.bfloat16)
    hidden = (activated * up_float).astype(jnp.bfloat16)
    return gate_grad, up_grad, hidden


def local(activations, out_grad, gate_pre, up_pre, gate_weight, up_weight, down_weight):
    odd = lax.axis_index("zh") % 2 == 1
    upper = lax.axis_index("core") == 1
    pre = gather_copies(jnp.concatenate([gate_pre, up_pre], axis=1), "zh", 4)
    tiles = to_features(jnp.stack([out_grad, activations]), odd)
    tiles, pre = lax.optimization_barrier((tiles, pre))
    mine, theirs = choose(upper, pre[64:], pre[:64])
    theirs = swap(theirs)
    pre = jnp.concatenate([mine[:, :512], theirs[:, :512], mine[:, 512:], theirs[:, 512:]], axis=1)
    pre = lax.all_gather(pre, "y", axis=0, tiled=True)
    cols = gather_copies(jnp.concatenate([tiles[0], tiles[1]], axis=1), PLANE, 8)
    grads, tokens = cols[:, :256], cols[:, 256:]
    down_both = jnp.concatenate([down_weight, swap(down_weight)], axis=0)
    gate_both = jnp.concatenate([gate_weight, swap(gate_weight)], axis=1)
    up_both = jnp.concatenate([up_weight, swap(up_weight)], axis=1)

    hidden_grad = scatter_sum(contract_cols(grads, down_both), ROW, R)
    hidden_grad, pre = lax.optimization_barrier((hidden_grad, pre))
    hidden_grad = gather_copies(hidden_grad, ROW, R)
    gate, up, hidden = swiglu_back(hidden_grad, pre[:, :1024], pre[:, 1024:])
    partial = contract_cols(gate, gate_both) + contract_cols(up, up_both)
    summed = scatter_sum(partial, PLANE, 8)
    cols_x = swap(cols)
    grads_x, tokens_x = cols_x[:, :256], cols_x[:, 256:]
    swapped = swap(jnp.concatenate([gate[:, 512:], up[:, 512:], hidden[:, 512:]], axis=1))
    summed, swapped = lax.optimization_barrier((summed, swapped))
    gate_x, up_x, hidden_x = swapped[:, :512], swapped[:, 512:1024], swapped[:, 1024:]
    input_grad = to_tokens(summed, odd)
    gate_weight_grad = contract_rows(tokens, gate[:, :512]) + contract_rows(tokens_x, gate_x)
    up_weight_grad = contract_rows(tokens, up[:, :512]) + contract_rows(tokens_x, up_x)
    down_weight_grad = contract_rows(hidden[:, :512], grads) + contract_rows(hidden_x, grads_x)
    return (
        input_grad,
        gate_weight_grad.astype(jnp.bfloat16),
        up_weight_grad.astype(jnp.bfloat16),
        down_weight_grad.astype(jnp.bfloat16),
    )


def solution(mesh):
    fine = Mesh(mesh.devices.reshape(8, 4, 4, 2, 2), AXES)
    return jax.shard_map(
        local,
        mesh=fine,
        in_specs=(P(ROW, COL),) * 6 + (P(COL, ROW),),
        out_specs=(P(ROW, COL),) * 3 + (P(COL, ROW),),
        check_vma=False,
    )
```

```python
import jax
import jax.numpy as jnp
from jax import lax
from jax.sharding import Mesh
from jax.sharding import PartitionSpec as P

AXES = ("yh", "yl", "zh", "x", "zl", "core")
ROW = ("yh", "yl", "zh")
ORDER = ("yl", "yh", "zh")
HALF = ("yh", "zh")
COL = ("x", "zl", "core")
PLANE = ("x", "zl")
R, C = 32, 16
TILES = [(t, t // 8, t // 4 % 2, t % 4) for t in range(R)]


def turn_in(half_of):
    return [
        (
            t * C + f,
            (f // 4 * 8 + yl * 4 + f % 2 * 2 + half_of(f // 2 % 2)) * C + yh * 4 + zh % 2 * 2 + zh // 2,
        )
        for t, yh, yl, zh in TILES
        for f in range(C)
    ]


def turn_out(half_of):
    return [
        ((2 * f + half_of(zh % 2)) * C + (yl * 2 + yh // 2) * 4 + yh % 2 * 2 + zh // 2, t * C + f)
        for t, yh, yl, zh in TILES
        for f in range(C)
    ]


IN_ONE, IN_TWO = turn_in(lambda b: b), turn_in(lambda b: 1 - b)
OUT_ONE, OUT_TWO = turn_out(lambda b: b), turn_out(lambda b: 1 - b)


def contract_rows(left, right):
    return lax.dot_general(
        left, right, (((0,), (0,)), ((), ())), preferred_element_type=jnp.float32
    )


def contract_cols(left, right):
    return lax.dot_general(
        left, right, (((1,), (1,)), ((), ())), preferred_element_type=jnp.float32
    )


def swap(value, axis="core"):
    return lax.ppermute(value, axis, [(0, 1), (1, 0)])


def choose(flag, one, other):
    return jnp.where(flag, one, other), jnp.where(flag, other, one)


def to_features(tile, upper, mine):
    one, two = choose(upper, tile[..., 256:], tile[..., :256])
    return choose(mine, lax.ppermute(one, AXES, IN_ONE), lax.ppermute(two, AXES, IN_TWO))


def to_tokens(piece, odd):
    one, two = choose(odd, piece[32:], piece[:32])
    high, low = choose(odd, lax.ppermute(one, AXES, OUT_ONE), lax.ppermute(two, AXES, OUT_TWO))
    return jnp.concatenate([low, high], axis=1)


def gather_copies(block, axes, size):
    copies = jnp.broadcast_to(block[None], (size,) + block.shape)
    got = lax.all_to_all(copies, axes, 0, 0, tiled=True)
    return got.reshape((size * block.shape[0],) + block.shape[1:])


def scatter_sum(partial, axes, size):
    pieces = partial.astype(jnp.bfloat16).reshape((size, partial.shape[0] // size, partial.shape[1]))
    got = lax.all_to_all(pieces, axes, 0, 0, tiled=True)
    return jnp.sum(got.astype(jnp.float32), axis=0).astype(jnp.bfloat16)


def swiglu_back(hidden_grad, gate_pre, up_pre):
    grad_float = hidden_grad.astype(jnp.float32)
    gate_float = gate_pre.astype(jnp.float32)
    up_float = up_pre.astype(jnp.float32)
    sigmoid_gate = jax.nn.sigmoid(gate_float)
    activated = gate_float * sigmoid_gate
    gate_grad = (
        grad_float * up_float * sigmoid_gate * (1.0 + gate_float * (1.0 - sigmoid_gate))
    ).astype(jnp.bfloat16)
    up_grad = (grad_float * activated).astype(jnp.bfloat16)
    hidden = (activated * up_float).astype(jnp.bfloat16)
    return gate_grad, up_grad, hidden


def local(activations, out_grad, gate_pre, up_pre, gate_weight, up_weight, down_weight):
    yl, zh, core = lax.axis_index("yl"), lax.axis_index("zh"), lax.axis_index("core")
    upper, mine, odd = lax.axis_index("zl") == 1, zh % 2 == yl, zh % 2 == 1
    pre = gather_copies(jnp.concatenate([gate_pre, up_pre], axis=1), "zh", 4)
    tiles = to_features(jnp.stack([out_grad, activations]), upper, mine)
    (own, other), pre, down_y = lax.optimization_barrier((tiles, pre, swap(down_weight, "yl")))
    pre = lax.all_gather(pre, ("yl", "yh"), axis=0, tiled=True)
    cols = gather_copies(jnp.concatenate([own[0], other[0], other[1], own[1]], axis=1), PLANE, 8)
    down = jnp.concatenate([down_weight, down_y], axis=1)
    down = jnp.concatenate([down, swap(down)], axis=0)
    partial = contract_cols(cols[:, :512], down).astype(jnp.bfloat16)
    hidden_grad = scatter_sum(partial, HALF, C)
    hidden_grad, pre, cols = lax.optimization_barrier((hidden_grad, pre, cols))

    hidden_grad = gather_copies(hidden_grad, ORDER, R)
    pre_mine, pre_theirs = choose(core == 1, *(pre.reshape(8, 2, 64, 1024)[:, at] for at in (1, 0)))
    pre_mine, pre_theirs = pre_mine.reshape(512, 1024), swap(pre_theirs.reshape(512, 1024))
    cols_y = swap(cols[:, 256:768], "yl")
    cols_own = jnp.concatenate([cols[:, :256], cols[:, 768:]], axis=1)
    cols = jnp.where(
        yl == 0,
        jnp.concatenate([cols_own, cols_y], axis=0),
        jnp.concatenate([cols_y, cols_own], axis=0),
    )
    hidden_grad, pre_mine, pre_theirs, gate_other, up_other, cols, cols_x = lax.optimization_barrier(
        (hidden_grad, pre_mine, pre_theirs, swap(gate_weight), swap(up_weight), cols, swap(cols))
    )
    gate, up, hidden = swiglu_back(hidden_grad[:, :512], pre_mine[:, :512], pre_mine[:, 512:])
    gate_y, up_y, hidden_y = swiglu_back(hidden_grad[:, 512:], pre_theirs[:, :512], pre_theirs[:, 512:])
    partial = contract_cols(gate, gate_weight) + contract_cols(up, up_weight)
    partial = partial + contract_cols(gate_y, gate_other) + contract_cols(up_y, up_other)
    summed = scatter_sum(partial, PLANE, 8)

    grads, tokens = cols[:, :256], cols[:, 256:]
    grads_x, tokens_x = cols_x[:, :256], cols_x[:, 256:]
    swapped = swap(jnp.concatenate([gate_y, up_y, hidden_y], axis=1))
    summed, swapped = lax.optimization_barrier((summed, swapped))
    gate_x, up_x, hidden_x = swapped[:, :512], swapped[:, 512:1024], swapped[:, 1024:]
    input_grad = to_tokens(summed, odd)
    gate_weight_grad = contract_rows(tokens, gate) + contract_rows(tokens_x, gate_x)
    up_weight_grad = contract_rows(tokens, up) + contract_rows(tokens_x, up_x)
    down_weight_grad = contract_rows(hidden, grads) + contract_rows(hidden_x, grads_x)
    return (
        input_grad,
        gate_weight_grad.astype(jnp.bfloat16),
        up_weight_grad.astype(jnp.bfloat16),
        down_weight_grad.astype(jnp.bfloat16),
    )


def solution(mesh):
    fine = Mesh(mesh.devices.reshape(4, 2, 4, 4, 2, 2), AXES)
    return jax.shard_map(
        local,
        mesh=fine,
        in_specs=(P(ROW, COL),) * 6 + (P(COL, ROW),),
        out_specs=(P(ROW, COL),) * 3 + (P(COL, ROW),),
        check_vma=False,
    )
```

```python
import jax
import jax.numpy as jnp
from jax import lax
from jax.sharding import Mesh
from jax.sharding import PartitionSpec as P

AXES = ("yh", "yl", "zh", "x", "zl", "core")
ROW = ("yh", "yl", "zh")
HALF = ("yh", "zh")
COL = ("x", "zl", "core")
PLANE = ("x", "zl")
R, C = 32, 16
TILES = [(t, t // 8, t // 4 % 2, t % 4) for t in range(R)]


def turn_in(half_of):
    return [
        (
            t * C + f,
            (f // 4 * 8 + yl * 4 + f % 2 * 2 + half_of(f // 2 % 2)) * C + yh * 4 + zh % 2 * 2 + zh // 2,
        )
        for t, yh, yl, zh in TILES
        for f in range(C)
    ]


def turn_out(half_of):
    return [
        ((2 * f + half_of(zh % 2)) * C + yh * 4 + yl * 2 + zh // 2, t * C + f)
        for t, yh, yl, zh in TILES
        for f in range(C)
    ]


IN_ONE, IN_TWO = turn_in(lambda b: b), turn_in(lambda b: 1 - b)
OUT_ONE, OUT_TWO = turn_out(lambda b: b), turn_out(lambda b: 1 - b)


def contract_rows(left, right):
    return lax.dot_general(
        left, right, (((0,), (0,)), ((), ())), preferred_element_type=jnp.float32
    )


def contract_cols(left, right):
    return lax.dot_general(
        left, right, (((1,), (1,)), ((), ())), preferred_element_type=jnp.float32
    )


def swap(value, axis="core"):
    return lax.ppermute(value, axis, [(0, 1), (1, 0)])


def choose(flag, one, other):
    return jnp.where(flag, one, other), jnp.where(flag, other, one)


def to_features(tile, upper, mine):
    one, two = choose(upper, tile[..., 256:], tile[..., :256])
    return choose(mine, lax.ppermute(one, AXES, IN_ONE), lax.ppermute(two, AXES, IN_TWO))


def to_tokens(piece, odd):
    one, two = choose(odd, piece[32:], piece[:32])
    high, low = choose(odd, lax.ppermute(one, AXES, OUT_ONE), lax.ppermute(two, AXES, OUT_TWO))
    return jnp.concatenate([low, high], axis=1)


def gather_copies(block, axes, size):
    copies = jnp.broadcast_to(block[None], (size,) + block.shape)
    got = lax.all_to_all(copies, axes, 0, 0, tiled=True)
    return got.reshape((size * block.shape[0],) + block.shape[1:])


def scatter_sum(partial, axes, size):
    pieces = partial.astype(jnp.bfloat16).reshape((size, partial.shape[0] // size, partial.shape[1]))
    got = lax.all_to_all(pieces, axes, 0, 0, tiled=True)
    return jnp.sum(got.astype(jnp.float32), axis=0).astype(jnp.bfloat16)


def swiglu_back(hidden_grad, gate_pre, up_pre):
    grad_float = hidden_grad.astype(jnp.float32)
    gate_float = gate_pre.astype(jnp.float32)
    up_float = up_pre.astype(jnp.float32)
    sigmoid_gate = jax.nn.sigmoid(gate_float)
    activated = gate_float * sigmoid_gate
    gate_grad = (
        grad_float * up_float * sigmoid_gate * (1.0 + gate_float * (1.0 - sigmoid_gate))
    ).astype(jnp.bfloat16)
    up_grad = (grad_float * activated).astype(jnp.bfloat16)
    hidden = (activated * up_float).astype(jnp.bfloat16)
    return gate_grad, up_grad, hidden


def local(activations, out_grad, gate_pre, up_pre, gate_weight, up_weight, down_weight):
    yl, zh, core = lax.axis_index("yl"), lax.axis_index("zh"), lax.axis_index("core")
    upper, mine, odd = lax.axis_index("zl") == 1, zh % 2 == yl, zh % 2 == 1
    pre = gather_copies(jnp.concatenate([gate_pre, up_pre], axis=1), "zh", 4)
    tiles = to_features(jnp.stack([out_grad, activations]), upper, mine)
    (own, other), pre, down_y = lax.optimization_barrier((tiles, pre, swap(down_weight, "yl")))
    pre = lax.all_gather(pre, ("yh", "yl"), axis=0, tiled=True)
    cols = gather_copies(jnp.concatenate([own[0], other[0], other[1], own[1]], axis=1), PLANE, 8)
    down = jnp.concatenate([down_weight, down_y], axis=1)
    down = jnp.concatenate([down, swap(down)], axis=0)
    partial = contract_cols(cols[:, :512], down).astype(jnp.bfloat16)
    hidden_grad = scatter_sum(partial, HALF, C)
    cols_y = swap(cols[:, 256:768], "yl")
    hidden_grad, pre, cols, cols_y = lax.optimization_barrier((hidden_grad, pre, cols, cols_y))

    hidden_grad = gather_copies(hidden_grad, ROW, R)
    pre_mine, pre_theirs = choose(core == 1, *(pre.reshape(8, 2, 64, 1024)[:, at] for at in (1, 0)))
    pre_mine, pre_theirs = pre_mine.reshape(512, 1024), swap(pre_theirs.reshape(512, 1024))
    cols = jnp.concatenate([cols[:, :256], cols[:, 768:]], axis=1).reshape(4, 64, 512)
    cols_y = cols_y.reshape(4, 64, 512)
    cols = jnp.stack(choose(yl == 0, cols, cols_y), axis=1).reshape(512, 512)
    hidden_grad, pre_mine, pre_theirs, gate_other, up_other, cols, cols_x = lax.optimization_barrier(
        (hidden_grad, pre_mine, pre_theirs, swap(gate_weight), swap(up_weight), cols, swap(cols))
    )
    gate, up, hidden = swiglu_back(hidden_grad[:, :512], pre_mine[:, :512], pre_mine[:, 512:])
    gate_y, up_y, hidden_y = swiglu_back(hidden_grad[:, 512:], pre_theirs[:, :512], pre_theirs[:, 512:])
    partial = contract_cols(gate, gate_weight) + contract_cols(up, up_weight)
    partial = partial + contract_cols(gate_y, gate_other) + contract_cols(up_y, up_other)
    summed = scatter_sum(partial, PLANE, 8)

    grads, tokens = cols[:, :256], cols[:, 256:]
    grads_x, tokens_x = cols_x[:, :256], cols_x[:, 256:]
    swapped = swap(jnp.concatenate([gate_y, up_y, hidden_y], axis=1))
    summed, swapped = lax.optimization_barrier((summed, swapped))
    gate_x, up_x, hidden_x = swapped[:, :512], swapped[:, 512:1024], swapped[:, 1024:]
    input_grad = to_tokens(summed, odd)
    gate_weight_grad = contract_rows(tokens, gate) + contract_rows(tokens_x, gate_x)
    up_weight_grad = contract_rows(tokens, up) + contract_rows(tokens_x, up_x)
    down_weight_grad = contract_rows(hidden, grads) + contract_rows(hidden_x, grads_x)
    return (
        input_grad,
        gate_weight_grad.astype(jnp.bfloat16),
        up_weight_grad.astype(jnp.bfloat16),
        down_weight_grad.astype(jnp.bfloat16),
    )


def solution(mesh):
    fine = Mesh(mesh.devices.reshape(4, 2, 4, 4, 2, 2), AXES)
    return jax.shard_map(
        local,
        mesh=fine,
        in_specs=(P(ROW, COL),) * 6 + (P(COL, ROW),),
        out_specs=(P(ROW, COL),) * 3 + (P(COL, ROW),),
        check_vma=False,
    )
```

```python
import jax
import jax.numpy as jnp
from jax import lax
from jax.sharding import Mesh
from jax.sharding import PartitionSpec as P

AXES = ("y", "zh", "x", "zl", "core")
ROW = ("y", "zh")
COL = ("x", "zl", "core")
PLANE = ("x", "zl")
R, C = 32, 16

SAME = [(t * C + f, (2 * f + t % 2) * C + t // 2) for t in range(R) for f in range(C)]
OTHER = [(t * C + f, (2 * f + 1 - t % 2) * C + t // 2) for t in range(R) for f in range(C)]


def inverse(pairs):
    return [(b, a) for a, b in pairs]


def contract_rows(left, right):
    return lax.dot_general(
        left, right, (((0,), (0,)), ((), ())), preferred_element_type=jnp.float32
    )


def contract_cols(left, right):
    return lax.dot_general(
        left, right, (((1,), (1,)), ((), ())), preferred_element_type=jnp.float32
    )


def swap(value):
    return lax.ppermute(value, "core", [(0, 1), (1, 0)])


def choose(flag, one, other):
    return jnp.where(flag, one, other), jnp.where(flag, other, one)


def to_features(tile, odd):
    one, two = choose(odd, tile[..., 256:], tile[..., :256])
    one = lax.ppermute(one, AXES, SAME)
    two = lax.ppermute(two, AXES, OTHER)
    second, first = choose(odd, one, two)
    return jnp.concatenate([first, second], axis=-2)


def to_tokens(piece, odd, beside):
    one, two = choose(odd, piece[32:], piece[:32])
    one = lax.ppermute(one, AXES, inverse(SAME))
    two = lax.ppermute(two, AXES, inverse(OTHER))
    one, two, beside = lax.optimization_barrier((one, two, beside))
    high, low = choose(odd, one, two)
    return (jnp.concatenate([low, high], axis=1),) + beside


def gather_copies(block, axes, size):
    copies = jnp.broadcast_to(block[None], (size,) + block.shape)
    got = lax.all_to_all(copies, axes, 0, 0, tiled=True)
    return got.reshape((size * block.shape[0],) + block.shape[1:])


def scatter_sum(partial, axes, size):
    pieces = partial.astype(jnp.bfloat16).reshape((size, partial.shape[0] // size, partial.shape[1]))
    got = lax.all_to_all(pieces, axes, 0, 0, tiled=True)
    return jnp.sum(got.astype(jnp.float32), axis=0).astype(jnp.bfloat16)


def swiglu_back(hidden_grad, gate_pre, up_pre):
    grad_float = hidden_grad.astype(jnp.float32)
    gate_float = gate_pre.astype(jnp.float32)
    up_float = up_pre.astype(jnp.float32)
    sigmoid_gate = jax.nn.sigmoid(gate_float)
    activated = gate_float * sigmoid_gate
    gate_grad = (
        grad_float * up_float * sigmoid_gate * (1.0 + gate_float * (1.0 - sigmoid_gate))
    ).astype(jnp.bfloat16)
    up_grad = (grad_float * activated).astype(jnp.bfloat16)
    hidden = (activated * up_float).astype(jnp.bfloat16)
    return gate_grad, up_grad, hidden


def local(activations, out_grad, gate_pre, up_pre, gate_weight, up_weight, down_weight):
    odd = lax.axis_index("zh") % 2 == 1
    upper = lax.axis_index("core") == 1
    pre = gather_copies(jnp.concatenate([gate_pre, up_pre], axis=1), "zh", 4)
    tiles = to_features(jnp.stack([out_grad, activations]), odd)
    tiles, pre = lax.optimization_barrier((tiles, pre))
    pre = lax.all_gather(pre, "y", axis=0, tiled=True)
    cols = gather_copies(jnp.concatenate([tiles[0], tiles[1]], axis=1), PLANE, 8)
    down_both = jnp.concatenate([down_weight, swap(down_weight)], axis=0)
    hidden_grad = scatter_sum(contract_cols(cols[:, :256], down_both), ROW, R)
    hidden_grad, pre, cols = lax.optimization_barrier((hidden_grad, pre, cols))

    hidden_grad = gather_copies(hidden_grad, ROW, R)
    pre = pre.reshape(8, 2, 64, 1024)
    pre_a, pre_b = choose(upper, pre[:, 1], pre[:, 0])
    pre_a, pre_b = pre_a.reshape(512, 1024), pre_b.reshape(512, 1024)
    hidden_grad, pre_a, pre_b, pre_y, gate_other, up_other, cols, cols_b = lax.optimization_barrier(
        (hidden_grad, pre_a, pre_b, swap(pre_b), swap(gate_weight), swap(up_weight), cols, swap(cols))
    )
    gate_a, up_a, hidden_a = swiglu_back(hidden_grad[:, :512], pre_a[:, :512], pre_a[:, 512:])
    gate_y, up_y, _ = swiglu_back(hidden_grad[:, 512:], pre_y[:, :512], pre_y[:, 512:])
    partial = contract_cols(gate_a, gate_weight) + contract_cols(up_a, up_weight)
    partial = partial + contract_cols(gate_y, gate_other) + contract_cols(up_y, up_other)
    summed = scatter_sum(partial, PLANE, 8)
    hidden_grad_b, pre_b = lax.optimization_barrier((swap(hidden_grad[:, 512:]), pre_b))
    gate_b, up_b, hidden_b = swiglu_back(hidden_grad_b, pre_b[:, :512], pre_b[:, 512:])
    grads_a, tokens_a = cols[:, :256], cols[:, 256:]
    grads_b, tokens_b = cols_b[:, :256], cols_b[:, 256:]
    products = contract_rows(tokens_a, gate_a), contract_rows(tokens_a, up_a), contract_rows(hidden_a, grads_a)
    summed, products = lax.optimization_barrier((summed, products))
    weight_grads = (
        (products[0] + contract_rows(tokens_b, gate_b)).astype(jnp.bfloat16),
        (products[1] + contract_rows(tokens_b, up_b)).astype(jnp.bfloat16),
        (products[2] + contract_rows(hidden_b, grads_b)).astype(jnp.bfloat16),
    )
    return to_tokens(summed, odd, weight_grads)


def solution(mesh):
    fine = Mesh(mesh.devices.reshape(8, 4, 4, 2, 2), AXES)
    return jax.shard_map(
        local,
        mesh=fine,
        in_specs=(P(ROW, COL),) * 6 + (P(COL, ROW),),
        out_specs=(P(ROW, COL),) * 3 + (P(COL, ROW),),
        check_vma=False,
    )
```

```python
import jax
import jax.numpy as jnp
from jax import lax
from jax.sharding import Mesh
from jax.sharding import PartitionSpec as P

AXES = ("yh", "yl", "zh", "x", "zl", "core")
ROW = ("yh", "yl", "zh")
HALF = ("yh", "zh")
COL = ("x", "zl", "core")
PLANE = ("x", "zl")
R, C = 32, 16
TILES = [(t, t // 8, t // 4 % 2, t % 4) for t in range(R)]


def turn_in(half_of):
    return [
        (
            t * C + f,
            (f // 4 * 8 + yl * 4 + f % 2 * 2 + half_of(f // 2 % 2)) * C + yh * 4 + zh % 2 * 2 + zh // 2,
        )
        for t, yh, yl, zh in TILES
        for f in range(C)
    ]


def turn_out(half_of):
    return [
        ((2 * f + half_of(zh % 2)) * C + yh * 4 + yl * 2 + zh // 2, t * C + f)
        for t, yh, yl, zh in TILES
        for f in range(C)
    ]


IN_ONE, IN_TWO = turn_in(lambda b: b), turn_in(lambda b: 1 - b)
OUT_ONE, OUT_TWO = turn_out(lambda b: b), turn_out(lambda b: 1 - b)


def contract_rows(left, right):
    return lax.dot_general(
        left, right, (((0,), (0,)), ((), ())), preferred_element_type=jnp.float32
    )


def contract_cols(left, right):
    return lax.dot_general(
        left, right, (((1,), (1,)), ((), ())), preferred_element_type=jnp.float32
    )


def swap(value, axis="core"):
    return lax.ppermute(value, axis, [(0, 1), (1, 0)])


def choose(flag, one, other):
    return jnp.where(flag, one, other), jnp.where(flag, other, one)


def to_features(tile, upper, mine):
    one, two = choose(upper, tile[..., 256:], tile[..., :256])
    return choose(mine, lax.ppermute(one, AXES, IN_ONE), lax.ppermute(two, AXES, IN_TWO))


def to_tokens(piece, odd, beside):
    one, two = choose(odd, piece[32:], piece[:32])
    one, two = lax.ppermute(one, AXES, OUT_ONE), lax.ppermute(two, AXES, OUT_TWO)
    one, two, beside = lax.optimization_barrier((one, two, beside))
    high, low = choose(odd, one, two)
    return (jnp.concatenate([low, high], axis=1),) + beside


def gather_copies(block, axes, size):
    copies = jnp.broadcast_to(block[None], (size,) + block.shape)
    got = lax.all_to_all(copies, axes, 0, 0, tiled=True)
    return got.reshape((size * block.shape[0],) + block.shape[1:])


def scatter_sum(partial, axes, size):
    pieces = partial.astype(jnp.bfloat16).reshape((size, partial.shape[0] // size, partial.shape[1]))
    got = lax.all_to_all(pieces, axes, 0, 0, tiled=True)
    return jnp.sum(got.astype(jnp.float32), axis=0).astype(jnp.bfloat16)


def swiglu_back(hidden_grad, gate_pre, up_pre):
    grad_float = hidden_grad.astype(jnp.float32)
    gate_float = gate_pre.astype(jnp.float32)
    up_float = up_pre.astype(jnp.float32)
    sigmoid_gate = jax.nn.sigmoid(gate_float)
    activated = gate_float * sigmoid_gate
    gate_grad = (
        grad_float * up_float * sigmoid_gate * (1.0 + gate_float * (1.0 - sigmoid_gate))
    ).astype(jnp.bfloat16)
    up_grad = (grad_float * activated).astype(jnp.bfloat16)
    hidden = (activated * up_float).astype(jnp.bfloat16)
    return gate_grad, up_grad, hidden


def local(activations, out_grad, gate_pre, up_pre, gate_weight, up_weight, down_weight):
    yl, zh, core = lax.axis_index("yl"), lax.axis_index("zh"), lax.axis_index("core")
    upper, mine, odd = lax.axis_index("zl") == 1, zh % 2 == yl, zh % 2 == 1
    pre = gather_copies(jnp.concatenate([gate_pre, up_pre], axis=1), "zh", 4)
    tiles = to_features(jnp.stack([out_grad, activations]), upper, mine)
    (own, other), pre, down_y = lax.optimization_barrier((tiles, pre, swap(down_weight, "yl")))
    pre = lax.all_gather(pre, ("yh", "yl"), axis=0, tiled=True)
    cols = gather_copies(jnp.concatenate([own[0], other[0], other[1], own[1]], axis=1), PLANE, 8)
    down = jnp.concatenate([down_weight, down_y], axis=1)
    down = jnp.concatenate([down, swap(down)], axis=0)
    partial = contract_cols(cols[:, :512], down).astype(jnp.bfloat16)
    hidden_grad = scatter_sum(partial, HALF, C)
    hidden_grad, pre, cols, gate_other, up_other = lax.optimization_barrier(
        (hidden_grad, pre, cols, swap(gate_weight), swap(up_weight))
    )

    hidden_grad = gather_copies(hidden_grad, ROW, R)
    pre = pre.reshape(8, 2, 64, 1024)
    pre_a, pre_b = choose(core == 1, pre[:, 1], pre[:, 0])
    pre_a, pre_b = pre_a.reshape(512, 1024), pre_b.reshape(512, 1024)
    cols_y = swap(cols[:, 256:768], "yl").reshape(4, 64, 512)
    cols = jnp.concatenate([cols[:, :256], cols[:, 768:]], axis=1).reshape(4, 64, 512)
    cols = jnp.stack(choose(yl == 0, cols, cols_y), axis=1).reshape(512, 512)
    hidden_grad, pre_a, pre_b, pre_y, cols = lax.optimization_barrier(
        (hidden_grad, pre_a, pre_b, swap(pre_b), cols)
    )
    cols_b = swap(cols)
    gate_a, up_a, hidden_a = swiglu_back(hidden_grad[:, :512], pre_a[:, :512], pre_a[:, 512:])
    gate_y, up_y, _ = swiglu_back(hidden_grad[:, 512:], pre_y[:, :512], pre_y[:, 512:])
    partial = contract_cols(gate_a, gate_weight) + contract_cols(up_a, up_weight)
    partial = partial + contract_cols(gate_y, gate_other) + contract_cols(up_y, up_other)
    summed = scatter_sum(partial, PLANE, 8)
    hidden_grad_b, pre_b = lax.optimization_barrier((swap(hidden_grad[:, 512:]), pre_b))
    gate_b, up_b, hidden_b = swiglu_back(hidden_grad_b, pre_b[:, :512], pre_b[:, 512:])
    grads_a, tokens_a = cols[:, :256], cols[:, 256:]
    grads_b, tokens_b = cols_b[:, :256], cols_b[:, 256:]
    products = contract_rows(tokens_a, gate_a), contract_rows(tokens_a, up_a), contract_rows(hidden_a, grads_a)
    summed, products = lax.optimization_barrier((summed, products))
    weight_grads = (
        (products[0] + contract_rows(tokens_b, gate_b)).astype(jnp.bfloat16),
        (products[1] + contract_rows(tokens_b, up_b)).astype(jnp.bfloat16),
        (products[2] + contract_rows(hidden_b, grads_b)).astype(jnp.bfloat16),
    )
    return to_tokens(summed, odd, weight_grads)


def solution(mesh):
    fine = Mesh(mesh.devices.reshape(4, 2, 4, 4, 2, 2), AXES)
    return jax.shard_map(
        local,
        mesh=fine,
        in_specs=(P(ROW, COL),) * 6 + (P(COL, ROW),),
        out_specs=(P(ROW, COL),) * 3 + (P(COL, ROW),),
        check_vma=False,
    )
```

```python
import jax
import jax.numpy as jnp
from jax import lax
from jax.sharding import Mesh
from jax.sharding import PartitionSpec as P

AXES = ("yh", "yl", "zh", "x", "zl", "core")
ROW = ("yh", "yl", "zh")
HALF = ("yh", "zh")
COL = ("x", "zl", "core")
PLANE = ("x", "zl")
R, C = 32, 16
TILES = [(t, t // 8, t // 4 % 2, t % 4) for t in range(R)]


def turn_in(half_of):
    return [
        (
            t * C + f,
            (f // 4 * 8 + yl * 4 + f % 2 * 2 + half_of(f // 2 % 2)) * C + yh * 4 + zh % 2 * 2 + zh // 2,
        )
        for t, yh, yl, zh in TILES
        for f in range(C)
    ]


def turn_out(half_of):
    return [
        ((2 * f + half_of(zh % 2)) * C + yh * 4 + yl * 2 + zh // 2, t * C + f)
        for t, yh, yl, zh in TILES
        for f in range(C)
    ]


IN_ONE, IN_TWO = turn_in(lambda b: b), turn_in(lambda b: 1 - b)
OUT_ONE, OUT_TWO = turn_out(lambda b: b), turn_out(lambda b: 1 - b)


def contract_rows(left, right):
    return lax.dot_general(
        left, right, (((0,), (0,)), ((), ())), preferred_element_type=jnp.float32
    )


def contract_cols(left, right):
    return lax.dot_general(
        left, right, (((1,), (1,)), ((), ())), preferred_element_type=jnp.float32
    )


def swap(value, axis="core"):
    return lax.ppermute(value, axis, [(0, 1), (1, 0)])


def choose(flag, one, other):
    return jnp.where(flag, one, other), jnp.where(flag, other, one)


def to_features(tile, upper, mine):
    one, two = choose(upper, tile[..., 256:], tile[..., :256])
    return choose(mine, lax.ppermute(one, AXES, IN_ONE), lax.ppermute(two, AXES, IN_TWO))


def to_tokens(piece, odd, beside):
    one, two = choose(odd, piece[32:], piece[:32])
    one, two = lax.ppermute(one, AXES, OUT_ONE), lax.ppermute(two, AXES, OUT_TWO)
    one, two, beside = lax.optimization_barrier((one, two, beside))
    high, low = choose(odd, one, two)
    return (jnp.concatenate([low, high], axis=1),) + beside


def gather_copies(block, axes, size):
    copies = jnp.broadcast_to(block[None], (size,) + block.shape)
    got = lax.all_to_all(copies, axes, 0, 0, tiled=True)
    return got.reshape((size * block.shape[0],) + block.shape[1:])


def scatter_sum(partial, axes, size):
    pieces = partial.astype(jnp.bfloat16).reshape((size, partial.shape[0] // size, partial.shape[1]))
    got = lax.all_to_all(pieces, axes, 0, 0, tiled=True)
    return jnp.sum(got.astype(jnp.float32), axis=0).astype(jnp.bfloat16)


def swiglu_back(hidden_grad, gate_pre, up_pre):
    grad_float = hidden_grad.astype(jnp.float32)
    gate_float = gate_pre.astype(jnp.float32)
    up_float = up_pre.astype(jnp.float32)
    sigmoid_gate = jax.nn.sigmoid(gate_float)
    activated = gate_float * sigmoid_gate
    gate_grad = (
        grad_float * up_float * sigmoid_gate * (1.0 + gate_float * (1.0 - sigmoid_gate))
    ).astype(jnp.bfloat16)
    up_grad = (grad_float * activated).astype(jnp.bfloat16)
    hidden = (activated * up_float).astype(jnp.bfloat16)
    return gate_grad, up_grad, hidden


def local(activations, out_grad, gate_pre, up_pre, gate_weight, up_weight, down_weight):
    yl, zh, core = lax.axis_index("yl"), lax.axis_index("zh"), lax.axis_index("core")
    upper, mine, odd = lax.axis_index("zl") == 1, zh % 2 == yl, zh % 2 == 1
    pre = gather_copies(jnp.concatenate([gate_pre, up_pre], axis=1), "zh", 4)
    tiles = to_features(jnp.stack([out_grad, activations]), upper, mine)
    (own, other), pre, down_y = lax.optimization_barrier((tiles, pre, swap(down_weight, "yl")))
    pre = lax.all_gather(pre, ("yh", "yl"), axis=0, tiled=True)
    cols = gather_copies(jnp.concatenate([own[0], other[0], other[1], own[1]], axis=1), PLANE, 8)
    down = jnp.concatenate([down_weight, down_y], axis=1)
    down = jnp.concatenate([down, swap(down)], axis=0)
    partial = contract_cols(cols[:, :512], down).astype(jnp.bfloat16)
    hidden_grad = scatter_sum(partial, HALF, C)
    hidden_grad, cols, gate_other, up_other = lax.optimization_barrier(
        (hidden_grad, cols, swap(gate_weight), swap(up_weight))
    )

    hidden_grad = gather_copies(hidden_grad, ROW, R)
    pre = pre.reshape(8, 2, 64, 1024)
    pre_a, pre_b = choose(core == 1, pre[:, 1], pre[:, 0])
    pre_a, pre_b = pre_a.reshape(512, 1024), pre_b.reshape(512, 1024)
    cols_y = swap(cols[:, 256:768], "yl").reshape(4, 64, 512)
    cols = jnp.concatenate([cols[:, :256], cols[:, 768:]], axis=1).reshape(4, 64, 512)
    cols = jnp.stack(choose(yl == 0, cols, cols_y), axis=1).reshape(512, 512)
    hidden_grad, pre_a, pre_b, pre_y, cols = lax.optimization_barrier(
        (hidden_grad, pre_a, pre_b, swap(pre_b), cols)
    )
    made_a = swiglu_back(hidden_grad[:, :512], pre_a[:, :512], pre_a[:, 512:])
    made_y = swiglu_back(hidden_grad[:, 512:], pre_y[:, :512], pre_y[:, 512:])[:2]
    (gate_a, up_a, hidden_a), (gate_y, up_y) = lax.optimization_barrier((made_a, made_y))
    partial = contract_cols(gate_a, gate_weight) + contract_cols(up_a, up_weight)
    partial = partial + contract_cols(gate_y, gate_other) + contract_cols(up_y, up_other)
    partial, cols, crossing = lax.optimization_barrier(
        (partial.astype(jnp.bfloat16), cols, hidden_grad[:, 512:])
    )
    summed = scatter_sum(partial, PLANE, 8)
    cols_b, crossed = swap(cols), swap(crossing)
    made_b = swiglu_back(crossed, pre_b[:, :512], pre_b[:, 512:])

    grads_a, tokens_a = cols[:, :256], cols[:, 256:]
    grads_b, tokens_b = cols_b[:, :256], cols_b[:, 256:]
    products = contract_rows(tokens_a, gate_a), contract_rows(tokens_a, up_a), contract_rows(hidden_a, grads_a)
    summed, products = lax.optimization_barrier((summed, products))
    gate_b, up_b, hidden_b = lax.optimization_barrier(made_b)
    weight_grads = (
        (products[0] + contract_rows(tokens_b, gate_b)).astype(jnp.bfloat16),
        (products[1] + contract_rows(tokens_b, up_b)).astype(jnp.bfloat16),
        (products[2] + contract_rows(hidden_b, grads_b)).astype(jnp.bfloat16),
    )
    return to_tokens(summed, odd, weight_grads)


def solution(mesh):
    fine = Mesh(mesh.devices.reshape(4, 2, 4, 4, 2, 2), AXES)
    return jax.shard_map(
        local,
        mesh=fine,
        in_specs=(P(ROW, COL),) * 6 + (P(COL, ROW),),
        out_specs=(P(ROW, COL),) * 3 + (P(COL, ROW),),
        check_vma=False,
    )
```

```python
import jax
import jax.numpy as jnp
from jax import lax
from jax.sharding import Mesh
from jax.sharding import PartitionSpec as P

AXES = ("yh", "yl", "zh", "x", "zl", "core")
ROW = ("yh", "yl", "zh")
HALF = ("yh", "zh")
COL = ("x", "zl", "core")
PLANE = ("x", "zl")
R, C = 32, 16
TILES = [(t, t // 8, t // 4 % 2, t % 4) for t in range(R)]


def turn_in(half_of):
    return [
        (
            t * C + f,
            (f // 4 * 8 + yl * 4 + f % 2 * 2 + half_of(f // 2 % 2)) * C + yh * 4 + zh % 2 * 2 + zh // 2,
        )
        for t, yh, yl, zh in TILES
        for f in range(C)
    ]


def turn_out(half_of):
    return [
        ((2 * f + half_of(zh % 2)) * C + yh * 4 + yl * 2 + zh // 2, t * C + f)
        for t, yh, yl, zh in TILES
        for f in range(C)
    ]


IN_ONE, IN_TWO = turn_in(lambda b: b), turn_in(lambda b: 1 - b)
OUT_ONE, OUT_TWO = turn_out(lambda b: b), turn_out(lambda b: 1 - b)


def contract_rows(left, right):
    return lax.dot_general(
        left, right, (((0,), (0,)), ((), ())), preferred_element_type=jnp.float32
    )


def contract_cols(left, right):
    return lax.dot_general(
        left, right, (((1,), (1,)), ((), ())), preferred_element_type=jnp.float32
    )


def swap(value, axis="core"):
    return lax.ppermute(value, axis, [(0, 1), (1, 0)])


def choose(flag, one, other):
    return jnp.where(flag, one, other), jnp.where(flag, other, one)


def to_features(tile, upper, mine):
    one, two = choose(upper, tile[..., 256:], tile[..., :256])
    return choose(mine, lax.ppermute(one, AXES, IN_ONE), lax.ppermute(two, AXES, IN_TWO))


def to_tokens(piece, odd, beside):
    one, two = choose(odd, piece[32:], piece[:32])
    one, two = lax.ppermute(one, AXES, OUT_ONE), lax.ppermute(two, AXES, OUT_TWO)
    one, two, beside = lax.optimization_barrier((one, two, beside))
    high, low = choose(odd, one, two)
    return (jnp.concatenate([low, high], axis=1),) + beside


def gather_copies(block, axes, size):
    copies = jnp.broadcast_to(block[None], (size,) + block.shape)
    got = lax.all_to_all(copies, axes, 0, 0, tiled=True)
    return got.reshape((size * block.shape[0],) + block.shape[1:])


def scatter_sum(partial, axes, size):
    pieces = partial.astype(jnp.bfloat16).reshape((size, partial.shape[0] // size, partial.shape[1]))
    got = lax.all_to_all(pieces, axes, 0, 0, tiled=True)
    return jnp.sum(got.astype(jnp.float32), axis=0).astype(jnp.bfloat16)


def slopes(gate_pre, up_pre):
    gate_float = gate_pre.astype(jnp.float32)
    up_float = up_pre.astype(jnp.float32)
    sigmoid_gate = jax.nn.sigmoid(gate_float)
    activated = gate_float * sigmoid_gate
    slope = up_float * sigmoid_gate * (1.0 + gate_float * (1.0 - sigmoid_gate))
    return slope, activated, (activated * up_float).astype(jnp.bfloat16)


def scaled(hidden_grad, slope, activated):
    grad_float = hidden_grad.astype(jnp.float32)
    return (grad_float * slope).astype(jnp.bfloat16), (grad_float * activated).astype(jnp.bfloat16)


def local(activations, out_grad, gate_pre, up_pre, gate_weight, up_weight, down_weight):
    yl, zh, core = lax.axis_index("yl"), lax.axis_index("zh"), lax.axis_index("core")
    upper, mine, odd = lax.axis_index("zl") == 1, zh % 2 == yl, zh % 2 == 1
    pre = gather_copies(jnp.concatenate([gate_pre, up_pre], axis=1), "zh", 4)
    tiles = to_features(jnp.stack([out_grad, activations]), upper, mine)
    (own, other), pre, down_y = lax.optimization_barrier((tiles, pre, swap(down_weight, "yl")))
    pre = lax.all_gather(pre, ("yh", "yl"), axis=0, tiled=True)
    cols = gather_copies(jnp.concatenate([own[0], other[0], other[1], own[1]], axis=1), PLANE, 8)
    down = jnp.concatenate([down_weight, down_y], axis=1)
    down = jnp.concatenate([down, swap(down)], axis=0)
    partial = contract_cols(cols[:, :512], down).astype(jnp.bfloat16)
    hidden_grad = scatter_sum(partial, HALF, C)
    hidden_grad, cols, gate_other, up_other = lax.optimization_barrier(
        (hidden_grad, cols, swap(gate_weight), swap(up_weight))
    )

    hidden_grad = gather_copies(hidden_grad, ROW, R)
    pre = pre.reshape(8, 2, 64, 1024)
    pre_a, pre_b = choose(core == 1, pre[:, 1], pre[:, 0])
    pre_a, pre_b = pre_a.reshape(512, 1024), pre_b.reshape(512, 1024)
    cols_y = swap(cols[:, 256:768], "yl")
    pre_y = swap(pre_b)
    slope_a, active_a, hidden_a = slopes(pre_a[:, :512], pre_a[:, 512:])
    slope_b, active_b, hidden_b = slopes(pre_b[:, :512], pre_b[:, 512:])
    slope_y, active_y, _ = slopes(pre_y[:, :512], pre_y[:, 512:])
    by_a, by_b, by_y, hidden_a, hidden_b, cols_y = lax.optimization_barrier(
        ((slope_a, active_a), (slope_b, active_b), (slope_y, active_y), hidden_a, hidden_b, cols_y)
    )
    cols = jnp.concatenate([cols[:, :256], cols[:, 768:]], axis=1).reshape(4, 64, 512)
    cols = jnp.stack(choose(yl == 0, cols, cols_y.reshape(4, 64, 512)), axis=1).reshape(512, 512)
    hidden_grad, cols, by_a, by_y = lax.optimization_barrier((hidden_grad, cols, by_a, by_y))
    made = scaled(hidden_grad[:, :512], *by_a), scaled(hidden_grad[:, 512:], *by_y)
    (gate_a, up_a), (gate_y, up_y) = lax.optimization_barrier(made)
    partial = contract_cols(gate_a, gate_weight) + contract_cols(up_a, up_weight)
    partial = partial + contract_cols(gate_y, gate_other) + contract_cols(up_y, up_other)
    partial, cols, crossing = lax.optimization_barrier(
        (partial.astype(jnp.bfloat16), cols, hidden_grad[:, 512:])
    )
    summed = scatter_sum(partial, PLANE, 8)
    cols_b = swap(cols)
    made_b = scaled(swap(crossing), *by_b)

    grads_a, tokens_a = cols[:, :256], cols[:, 256:]
    grads_b, tokens_b = cols_b[:, :256], cols_b[:, 256:]
    products = contract_rows(tokens_a, gate_a), contract_rows(tokens_a, up_a), contract_rows(hidden_a, grads_a)
    summed, products = lax.optimization_barrier((summed, products))
    gate_b, up_b = lax.optimization_barrier(made_b)
    weight_grads = (
        (products[0] + contract_rows(tokens_b, gate_b)).astype(jnp.bfloat16),
        (products[1] + contract_rows(tokens_b, up_b)).astype(jnp.bfloat16),
        (products[2] + contract_rows(hidden_b, grads_b)).astype(jnp.bfloat16),
    )
    return to_tokens(summed, odd, weight_grads)


def solution(mesh):
    fine = Mesh(mesh.devices.reshape(4, 2, 4, 4, 2, 2), AXES)
    return jax.shard_map(
        local,
        mesh=fine,
        in_specs=(P(ROW, COL),) * 6 + (P(COL, ROW),),
        out_specs=(P(ROW, COL),) * 3 + (P(COL, ROW),),
        check_vma=False,
    )
```

```python
import jax
import jax.numpy as jnp
from jax import lax
from jax.sharding import Mesh
from jax.sharding import PartitionSpec as P

AXES = ("yh", "yl", "zh", "x", "zl", "core")
ROW = ("yh", "yl", "zh")
HALF = ("yh", "zh")
COL = ("x", "zl", "core")
PLANE = ("x", "zl")
R, C = 32, 16
TILES = [(t, t // 8, t // 4 % 2, t % 4) for t in range(R)]


def turn_in(half_of):
    return [
        (
            t * C + f,
            (f // 4 * 8 + yl * 4 + f % 2 * 2 + half_of(f // 2 % 2)) * C + yh * 4 + zh % 2 * 2 + zh // 2,
        )
        for t, yh, yl, zh in TILES
        for f in range(C)
    ]


def turn_out(half_of):
    return [
        ((2 * f + half_of(zh % 2)) * C + yh * 4 + yl * 2 + zh // 2, t * C + f)
        for t, yh, yl, zh in TILES
        for f in range(C)
    ]


IN_ONE, IN_TWO = turn_in(lambda b: b), turn_in(lambda b: 1 - b)
OUT_ONE, OUT_TWO = turn_out(lambda b: b), turn_out(lambda b: 1 - b)


def contract_rows(left, right):
    return lax.dot_general(
        left, right, (((0,), (0,)), ((), ())), preferred_element_type=jnp.float32
    )


def contract_cols(left, right):
    return lax.dot_general(
        left, right, (((1,), (1,)), ((), ())), preferred_element_type=jnp.float32
    )


def swap(value, axis="core"):
    return lax.ppermute(value, axis, [(0, 1), (1, 0)])


def choose(flag, one, other):
    return jnp.where(flag, one, other), jnp.where(flag, other, one)


def to_features(tile, upper, mine):
    one, two = choose(upper, tile[..., 256:], tile[..., :256])
    return choose(mine, lax.ppermute(one, AXES, IN_ONE), lax.ppermute(two, AXES, IN_TWO))


def to_tokens(piece, odd, beside):
    one, two = choose(odd, piece[32:], piece[:32])
    one, two = lax.ppermute(one, AXES, OUT_ONE), lax.ppermute(two, AXES, OUT_TWO)
    one, two, beside = lax.optimization_barrier((one, two, beside))
    high, low = choose(odd, one, two)
    return (jnp.concatenate([low, high], axis=1),) + beside


def gather_copies(block, axes, size):
    copies = jnp.broadcast_to(block[None], (size,) + block.shape)
    got = lax.all_to_all(copies, axes, 0, 0, tiled=True)
    return got.reshape((size * block.shape[0],) + block.shape[1:])


def scatter_sum(partial, axes, size):
    pieces = partial.astype(jnp.bfloat16).reshape((size, partial.shape[0] // size, partial.shape[1]))
    got = lax.all_to_all(pieces, axes, 0, 0, tiled=True)
    return jnp.sum(got.astype(jnp.float32), axis=0).astype(jnp.bfloat16)


def slopes(gate_pre, up_pre):
    gate_float = gate_pre.astype(jnp.float32)
    up_float = up_pre.astype(jnp.float32)
    sigmoid_gate = jax.nn.sigmoid(gate_float)
    activated = gate_float * sigmoid_gate
    slope = up_float * sigmoid_gate * (1.0 + gate_float * (1.0 - sigmoid_gate))
    return slope, activated, (activated * up_float).astype(jnp.bfloat16)


def scaled(hidden_grad, slope, activated):
    grad_float = hidden_grad.astype(jnp.float32)
    return (grad_float * slope).astype(jnp.bfloat16), (grad_float * activated).astype(jnp.bfloat16)


def local(activations, out_grad, gate_pre, up_pre, gate_weight, up_weight, down_weight):
    yl, zh, core = lax.axis_index("yl"), lax.axis_index("zh"), lax.axis_index("core")
    upper, mine, odd = lax.axis_index("zl") == 1, zh % 2 == yl, zh % 2 == 1
    pre = lax.all_gather(jnp.concatenate([gate_pre, up_pre], axis=1), ROW, axis=0, tiled=True)
    tiles = to_features(jnp.stack([out_grad, activations]), upper, mine)
    (own, other), down_y = lax.optimization_barrier((tiles, swap(down_weight, "yl")))
    cols = gather_copies(jnp.concatenate([own[0], other[0], other[1], own[1]], axis=1), PLANE, 8)
    down = jnp.concatenate([down_weight, down_y], axis=1)
    down = jnp.concatenate([down, swap(down)], axis=0)
    partial = contract_cols(cols[:, :512], down).astype(jnp.bfloat16)
    hidden_grad = scatter_sum(partial, HALF, C)
    hidden_grad, cols, gate_other, up_other = lax.optimization_barrier(
        (hidden_grad, cols, swap(gate_weight), swap(up_weight))
    )

    hidden_grad = gather_copies(hidden_grad, ROW, R)
    pre = pre.reshape(8, 2, 64, 1024)
    pre_a, pre_b = choose(core == 1, pre[:, 1], pre[:, 0])
    pre_a, pre_b = pre_a.reshape(512, 1024), pre_b.reshape(512, 1024)
    cols_y = swap(cols[:, 256:768], "yl")
    pre_y = swap(pre_b)
    slope_a, active_a, hidden_a = slopes(pre_a[:, :512], pre_a[:, 512:])
    slope_b, active_b, hidden_b = slopes(pre_b[:, :512], pre_b[:, 512:])
    slope_y, active_y, _ = slopes(pre_y[:, :512], pre_y[:, 512:])
    by_a, by_b, by_y, hidden_a, hidden_b, cols_y = lax.optimization_barrier(
        ((slope_a, active_a), (slope_b, active_b), (slope_y, active_y), hidden_a, hidden_b, cols_y)
    )
    cols = jnp.concatenate([cols[:, :256], cols[:, 768:]], axis=1).reshape(4, 64, 512)
    cols = jnp.stack(choose(yl == 0, cols, cols_y.reshape(4, 64, 512)), axis=1).reshape(512, 512)
    hidden_grad, cols, by_a, by_y = lax.optimization_barrier((hidden_grad, cols, by_a, by_y))
    made = scaled(hidden_grad[:, :512], *by_a), scaled(hidden_grad[:, 512:], *by_y)
    (gate_a, up_a), (gate_y, up_y) = lax.optimization_barrier(made)
    partial = contract_cols(gate_a, gate_weight) + contract_cols(up_a, up_weight)
    partial = partial + contract_cols(gate_y, gate_other) + contract_cols(up_y, up_other)
    partial, cols, crossing = lax.optimization_barrier(
        (partial.astype(jnp.bfloat16), cols, hidden_grad[:, 512:])
    )
    summed = scatter_sum(partial, PLANE, 8)
    cols_b = swap(cols)
    made_b = scaled(swap(crossing), *by_b)

    grads_a, tokens_a = cols[:, :256], cols[:, 256:]
    grads_b, tokens_b = cols_b[:, :256], cols_b[:, 256:]
    products = contract_rows(tokens_a, gate_a), contract_rows(tokens_a, up_a), contract_rows(hidden_a, grads_a)
    summed, products = lax.optimization_barrier((summed, products))
    gate_b, up_b = lax.optimization_barrier(made_b)
    rest = lax.optimization_barrier(
        (contract_rows(tokens_b, gate_b), contract_rows(tokens_b, up_b), contract_rows(hidden_b, grads_b))
    )
    weight_grads = tuple((one + two).astype(jnp.bfloat16) for one, two in zip(products, rest))
    return to_tokens(summed, odd, weight_grads)


def solution(mesh):
    fine = Mesh(mesh.devices.reshape(4, 2, 4, 4, 2, 2), AXES)
    return jax.shard_map(
        local,
        mesh=fine,
        in_specs=(P(ROW, COL),) * 6 + (P(COL, ROW),),
        out_specs=(P(ROW, COL),) * 3 + (P(COL, ROW),),
        check_vma=False,
    )
```

```python
import jax
import jax.numpy as jnp
from jax import lax
from jax.sharding import Mesh
from jax.sharding import PartitionSpec as P

AXES = ("yh", "yl", "zh", "x", "zl", "core")
ROW = ("yh", "yl", "zh")
HALF = ("yh", "zh")
COL = ("x", "zl", "core")
PLANE = ("x", "zl")
R, C = 32, 16
TILES = [(t, t // 8, t // 4 % 2, t % 4) for t in range(R)]


def turn_in(half_of):
    return [
        (
            t * C + f,
            (f // 4 * 8 + yl * 4 + f % 2 * 2 + half_of(f // 2 % 2)) * C + yh * 4 + zh % 2 * 2 + zh // 2,
        )
        for t, yh, yl, zh in TILES
        for f in range(C)
    ]


def turn_out(half_of):
    return [
        ((2 * f + half_of(zh % 2)) * C + yh * 4 + yl * 2 + zh // 2, t * C + f)
        for t, yh, yl, zh in TILES
        for f in range(C)
    ]


IN_ONE, IN_TWO = turn_in(lambda b: b), turn_in(lambda b: 1 - b)
OUT_ONE, OUT_TWO = turn_out(lambda b: b), turn_out(lambda b: 1 - b)


def contract_rows(left, right):
    return lax.dot_general(
        left, right, (((0,), (0,)), ((), ())), preferred_element_type=jnp.float32
    )


def contract_cols(left, right):
    return lax.dot_general(
        left, right, (((1,), (1,)), ((), ())), preferred_element_type=jnp.float32
    )


def swap(value, axis="core"):
    return lax.ppermute(value, axis, [(0, 1), (1, 0)])


def choose(flag, one, other):
    return jnp.where(flag, one, other), jnp.where(flag, other, one)


def to_features(tile, upper, mine):
    one, two = choose(upper, tile[..., 256:], tile[..., :256])
    return choose(mine, lax.ppermute(one, AXES, IN_ONE), lax.ppermute(two, AXES, IN_TWO))


def to_tokens(piece, odd, beside):
    one, two = choose(odd, piece[32:], piece[:32])
    one, two = lax.ppermute(one, AXES, OUT_ONE), lax.ppermute(two, AXES, OUT_TWO)
    one, two, beside = lax.optimization_barrier((one, two, beside))
    high, low = choose(odd, one, two)
    return (jnp.concatenate([low, high], axis=1),) + beside


def gather_copies(block, axes, size):
    copies = jnp.broadcast_to(block[None], (size,) + block.shape)
    got = lax.all_to_all(copies, axes, 0, 0, tiled=True)
    return got.reshape((size * block.shape[0],) + block.shape[1:])


def scatter_sum(partial, axes, size):
    pieces = partial.astype(jnp.bfloat16).reshape((size, partial.shape[0] // size, partial.shape[1]))
    got = lax.all_to_all(pieces, axes, 0, 0, tiled=True)
    return jnp.sum(got.astype(jnp.float32), axis=0).astype(jnp.bfloat16)


def slopes(gate_pre, up_pre):
    gate_float = gate_pre.astype(jnp.float32)
    up_float = up_pre.astype(jnp.float32)
    sigmoid_gate = jax.nn.sigmoid(gate_float)
    activated = gate_float * sigmoid_gate
    slope = up_float * sigmoid_gate * (1.0 + gate_float * (1.0 - sigmoid_gate))
    return slope, activated, (activated * up_float).astype(jnp.bfloat16)


def scaled(hidden_grad, slope, activated):
    grad_float = hidden_grad.astype(jnp.float32)
    return (grad_float * slope).astype(jnp.bfloat16), (grad_float * activated).astype(jnp.bfloat16)


def local(activations, out_grad, gate_pre, up_pre, gate_weight, up_weight, down_weight):
    yl, zh, core = lax.axis_index("yl"), lax.axis_index("zh"), lax.axis_index("core")
    upper, mine, odd = lax.axis_index("zl") == 1, zh % 2 == yl, zh % 2 == 1
    pre = jnp.concatenate([gate_pre, up_pre], axis=1)
    tiles = to_features(jnp.stack([out_grad, activations]), upper, mine)
    (own, other), pre_x, down_y = lax.optimization_barrier(
        (tiles, swap(pre, "yl"), swap(down_weight, "yl"))
    )
    pre = jnp.concatenate(choose(yl == 0, pre, pre_x), axis=0)
    pre = lax.all_gather(pre, HALF, axis=0, tiled=True)
    cols = gather_copies(jnp.concatenate([own[0], other[0], other[1], own[1]], axis=1), PLANE, 8)
    down = jnp.concatenate([down_weight, down_y], axis=1)
    down = jnp.concatenate([down, swap(down)], axis=0)
    partial = contract_cols(cols[:, :512], down).astype(jnp.bfloat16)
    hidden_grad = scatter_sum(partial, HALF, C)
    hidden_grad, cols, gate_other, up_other = lax.optimization_barrier(
        (hidden_grad, cols, swap(gate_weight), swap(up_weight))
    )

    hidden_grad = gather_copies(hidden_grad, ROW, R)
    pre = pre.reshape(4, 2, 2, 2, 32, 1024)
    pre = tuple(pre[:, at].transpose(0, 2, 1, 3, 4).reshape(512, 1024) for at in (1, 0))
    pre_a, pre_b = choose(core == 1, *pre)
    cols_y = swap(cols[:, 256:768], "yl")
    pre_y = swap(pre_b)
    slope_a, active_a, hidden_a = slopes(pre_a[:, :512], pre_a[:, 512:])
    slope_b, active_b, hidden_b = slopes(pre_b[:, :512], pre_b[:, 512:])
    slope_y, active_y, _ = slopes(pre_y[:, :512], pre_y[:, 512:])
    by_a, by_b, by_y, hidden_a, hidden_b, cols_y = lax.optimization_barrier(
        ((slope_a, active_a), (slope_b, active_b), (slope_y, active_y), hidden_a, hidden_b, cols_y)
    )
    cols = jnp.concatenate([cols[:, :256], cols[:, 768:]], axis=1).reshape(4, 64, 512)
    cols = jnp.stack(choose(yl == 0, cols, cols_y.reshape(4, 64, 512)), axis=1).reshape(512, 512)
    hidden_grad, cols, by_a, by_y = lax.optimization_barrier((hidden_grad, cols, by_a, by_y))
    made = scaled(hidden_grad[:, :512], *by_a), scaled(hidden_grad[:, 512:], *by_y)
    (gate_a, up_a), (gate_y, up_y) = lax.optimization_barrier(made)
    partial = contract_cols(gate_a, gate_weight) + contract_cols(up_a, up_weight)
    partial = partial + contract_cols(gate_y, gate_other) + contract_cols(up_y, up_other)
    partial, cols, crossing = lax.optimization_barrier(
        (partial.astype(jnp.bfloat16), cols, hidden_grad[:, 512:])
    )
    summed = scatter_sum(partial, PLANE, 8)
    cols_b = swap(cols)
    made_b = scaled(swap(crossing), *by_b)

    grads_a, tokens_a = cols[:, :256], cols[:, 256:]
    grads_b, tokens_b = cols_b[:, :256], cols_b[:, 256:]
    products = contract_rows(tokens_a, gate_a), contract_rows(tokens_a, up_a), contract_rows(hidden_a, grads_a)
    summed, products = lax.optimization_barrier((summed, products))
    gate_b, up_b = lax.optimization_barrier(made_b)
    weight_grads = (
        (products[0] + contract_rows(tokens_b, gate_b)).astype(jnp.bfloat16),
        (products[1] + contract_rows(tokens_b, up_b)).astype(jnp.bfloat16),
        (products[2] + contract_rows(hidden_b, grads_b)).astype(jnp.bfloat16),
    )
    return to_tokens(summed, odd, weight_grads)


def solution(mesh):
    fine = Mesh(mesh.devices.reshape(4, 2, 4, 4, 2, 2), AXES)
    return jax.shard_map(
        local,
        mesh=fine,
        in_specs=(P(ROW, COL),) * 6 + (P(COL, ROW),),
        out_specs=(P(ROW, COL),) * 3 + (P(COL, ROW),),
        check_vma=False,
    )
```

```python
import jax
import jax.numpy as jnp
from jax import lax
from jax.sharding import Mesh
from jax.sharding import PartitionSpec as P

AXES = ("yh", "yl", "zh", "x", "zl", "core")
ROW = ("yh", "yl", "zh")
HALF = ("yh", "zh")
COL = ("x", "zl", "core")
PLANE = ("x", "zl")
R, C = 32, 16
TILES = [(t, t // 8, t // 4 % 2, t % 4) for t in range(R)]


def turn_in(half_of):
    return [
        (
            t * C + f,
            (f // 4 * 8 + yl * 4 + f % 2 * 2 + half_of(f // 2 % 2)) * C + yh * 4 + zh % 2 * 2 + zh // 2,
        )
        for t, yh, yl, zh in TILES
        for f in range(C)
    ]


def turn_out(half_of):
    return [
        ((2 * f + half_of(zh % 2)) * C + yh * 4 + yl * 2 + zh // 2, t * C + f)
        for t, yh, yl, zh in TILES
        for f in range(C)
    ]


IN_ONE, IN_TWO = turn_in(lambda b: b), turn_in(lambda b: 1 - b)
OUT_ONE, OUT_TWO = turn_out(lambda b: b), turn_out(lambda b: 1 - b)


def contract_rows(left, right):
    return lax.dot_general(
        left, right, (((0,), (0,)), ((), ())), preferred_element_type=jnp.float32
    )


def contract_cols(left, right):
    return lax.dot_general(
        left, right, (((1,), (1,)), ((), ())), preferred_element_type=jnp.float32
    )


def swap(value, axis="core"):
    return lax.ppermute(value, axis, [(0, 1), (1, 0)])


def choose(flag, one, other):
    return jnp.where(flag, one, other), jnp.where(flag, other, one)


def to_features(tile, upper, mine):
    one, two = choose(upper, tile[..., 256:], tile[..., :256])
    return choose(mine, lax.ppermute(one, AXES, IN_ONE), lax.ppermute(two, AXES, IN_TWO))


def to_tokens(piece, odd, beside):
    one, two = choose(odd, piece[32:], piece[:32])
    one, two = lax.ppermute(one, AXES, OUT_ONE), lax.ppermute(two, AXES, OUT_TWO)
    one, two, beside = lax.optimization_barrier((one, two, beside))
    high, low = choose(odd, one, two)
    return (jnp.concatenate([low, high], axis=1),) + beside


def gather_copies(block, axes, size):
    copies = jnp.broadcast_to(block[None], (size,) + block.shape)
    got = lax.all_to_all(copies, axes, 0, 0, tiled=True)
    return got.reshape((size * block.shape[0],) + block.shape[1:])


def scatter_sum(partial, axes, size):
    pieces = partial.astype(jnp.bfloat16).reshape((size, partial.shape[0] // size, partial.shape[1]))
    got = lax.all_to_all(pieces, axes, 0, 0, tiled=True)
    return jnp.sum(got.astype(jnp.float32), axis=0).astype(jnp.bfloat16)


def slopes(gate_pre, up_pre):
    gate_float = gate_pre.astype(jnp.float32)
    up_float = up_pre.astype(jnp.float32)
    sigmoid_gate = jax.nn.sigmoid(gate_float)
    activated = gate_float * sigmoid_gate
    slope = up_float * sigmoid_gate * (1.0 + gate_float * (1.0 - sigmoid_gate))
    return slope, activated, (activated * up_float).astype(jnp.bfloat16)


def scaled(hidden_grad, slope, activated):
    grad_float = hidden_grad.astype(jnp.float32)
    return (grad_float * slope).astype(jnp.bfloat16), (grad_float * activated).astype(jnp.bfloat16)


def local(activations, out_grad, gate_pre, up_pre, gate_weight, up_weight, down_weight):
    yl, zh, core = lax.axis_index("yl"), lax.axis_index("zh"), lax.axis_index("core")
    upper, mine, odd = lax.axis_index("zl") == 1, zh % 2 == yl, zh % 2 == 1
    pre = jnp.concatenate([gate_pre, up_pre], axis=1)
    others = tuple(
        lax.ppermute(pre, "zh", [(at, (at - step) % 4) for at in range(4)]) for step in (1, 2, 3)
    )
    tiles = to_features(jnp.stack([out_grad, activations]), upper, mine)
    (own, other), others, down_y = lax.optimization_barrier(
        (tiles, others, swap(down_weight, "yl"))
    )
    pre = jnp.stack((pre,) + others)
    pre = jnp.where(odd, jnp.concatenate([pre[3:], pre[:3]]), pre)
    pre = jnp.where(zh >= 2, jnp.concatenate([pre[2:], pre[:2]]), pre).reshape(128, 1024)
    pre = lax.all_gather(pre, ("yh", "yl"), axis=0, tiled=True)
    cols = gather_copies(jnp.concatenate([own[0], other[0], other[1], own[1]], axis=1), PLANE, 8)
    down = jnp.concatenate([down_weight, down_y], axis=1)
    down = jnp.concatenate([down, swap(down)], axis=0)
    partial = contract_cols(cols[:, :512], down).astype(jnp.bfloat16)
    hidden_grad = scatter_sum(partial, HALF, C)
    hidden_grad, cols, gate_other, up_other = lax.optimization_barrier(
        (hidden_grad, cols, swap(gate_weight), swap(up_weight))
    )

    hidden_grad = gather_copies(hidden_grad, ROW, R)
    pre = pre.reshape(8, 2, 64, 1024)
    pre_a, pre_b = choose(core == 1, pre[:, 1], pre[:, 0])
    pre_a, pre_b = pre_a.reshape(512, 1024), pre_b.reshape(512, 1024)
    cols_y = swap(cols[:, 256:768], "yl")
    pre_y = swap(pre_b)
    slope_a, active_a, hidden_a = slopes(pre_a[:, :512], pre_a[:, 512:])
    slope_b, active_b, hidden_b = slopes(pre_b[:, :512], pre_b[:, 512:])
    slope_y, active_y, _ = slopes(pre_y[:, :512], pre_y[:, 512:])
    by_a, by_b, by_y, hidden_a, hidden_b, cols_y = lax.optimization_barrier(
        ((slope_a, active_a), (slope_b, active_b), (slope_y, active_y), hidden_a, hidden_b, cols_y)
    )
    cols = jnp.concatenate([cols[:, :256], cols[:, 768:]], axis=1).reshape(4, 64, 512)
    cols = jnp.stack(choose(yl == 0, cols, cols_y.reshape(4, 64, 512)), axis=1).reshape(512, 512)
    hidden_grad, cols, by_a, by_y = lax.optimization_barrier((hidden_grad, cols, by_a, by_y))
    made = scaled(hidden_grad[:, :512], *by_a), scaled(hidden_grad[:, 512:], *by_y)
    (gate_a, up_a), (gate_y, up_y) = lax.optimization_barrier(made)
    partial = contract_cols(gate_a, gate_weight) + contract_cols(up_a, up_weight)
    partial = partial + contract_cols(gate_y, gate_other) + contract_cols(up_y, up_other)
    partial, cols, crossing = lax.optimization_barrier(
        (partial.astype(jnp.bfloat16), cols, hidden_grad[:, 512:])
    )
    summed = scatter_sum(partial, PLANE, 8)
    cols_b = swap(cols)
    made_b = scaled(swap(crossing), *by_b)

    grads_a, tokens_a = cols[:, :256], cols[:, 256:]
    grads_b, tokens_b = cols_b[:, :256], cols_b[:, 256:]
    products = contract_rows(tokens_a, gate_a), contract_rows(tokens_a, up_a), contract_rows(hidden_a, grads_a)
    summed, products = lax.optimization_barrier((summed, products))
    gate_b, up_b = lax.optimization_barrier(made_b)
    weight_grads = (
        (products[0] + contract_rows(tokens_b, gate_b)).astype(jnp.bfloat16),
        (products[1] + contract_rows(tokens_b, up_b)).astype(jnp.bfloat16),
        (products[2] + contract_rows(hidden_b, grads_b)).astype(jnp.bfloat16),
    )
    return to_tokens(summed, odd, weight_grads)


def solution(mesh):
    fine = Mesh(mesh.devices.reshape(4, 2, 4, 4, 2, 2), AXES)
    return jax.shard_map(
        local,
        mesh=fine,
        in_specs=(P(ROW, COL),) * 6 + (P(COL, ROW),),
        out_specs=(P(ROW, COL),) * 3 + (P(COL, ROW),),
        check_vma=False,
    )
```
